128 devices in a mesh: gx: 8 (over z_hi, y), gy: 16 (over z_lo, x, core).
Axes of the slice: x: 4, y: 4, z: 4 (z_hi: 2, z_lo: 2; z = z_hi * 2 + z_lo), core: 2. Of those that a mesh axis runs over, the one named last changes fastest.
Arguments:
- tokens: bfloat16 [32768, 1024], P(('gx', 'gy')), may hold values from -6 to 6
- ln1_gain: float32 [1024], replicated, may hold values from 0.5 to 1.5
- ln1_bias: float32 [1024], replicated, may hold values from -1.75 to 1.75
- w_qkv: bfloat16 [1024, 16, 192], P('gx', 'gy'), may hold values from -0.1875 to 0.1875
- b_qv: float32 [16, 128], P('gy'), may hold values from -1.75 to 1.75
- w_out: bfloat16 [16, 64, 1024], P('gy', None, 'gx'), may hold values from -1.5 to 1.5
- b_out: float32 [1024], replicated, may hold values from -1.75 to 1.75
- ln2_gain: float32 [1024], replicated, may hold values from 0.5 to 1.5
- ln2_bias: float32 [1024], replicated, may hold values from -1.75 to 1.75
- w_fc: bfloat16 [1024, 4096], P('gx', 'gy'), may hold values from -0.1875 to 0.1875
- b_fc: float32 [4096], P('gy'), may hold values from -3 to 3
- w_proj: bfloat16 [4096, 1024], P('gy', 'gx'), may hold values from -0.125 to 0.125
- b_proj: float32 [1024], replicated, may hold values from -1.75 to 1.75
- lengths: int32 [8, 3], P('gx'), may hold values from 1024 to 2048, as said below
- cotangent: bfloat16 [32768, 1024], P(('gx', 'gy')), may hold values from -6 to 6
Outputs:
- activations: bfloat16 [32768, 1024], P(('gx', 'gy'))
- input_grad: float32 [32768, 1024], P(('gx', 'gy'))
- grad_ln1_gain: float32 [1024], replicated
- grad_ln1_bias: float32 [1024], replicated
- grad_w_qkv: float32 [1024, 16, 192], P('gx', 'gy')
- grad_b_qv: float32 [16, 128], P('gy')
- grad_w_out: float32 [16, 64, 1024], P('gy', None, 'gx')
- grad_b_out: float32 [1024], replicated
- grad_ln2_gain: float32 [1024], replicated
- grad_ln2_bias: float32 [1024], replicated
- grad_w_fc: float32 [1024, 4096], P('gx', 'gy')
- grad_b_fc: float32 [4096], P('gy')
- grad_w_proj: float32 [4096, 1024], P('gy', 'gx')
- grad_b_proj: float32 [1024], replicated
The draws below stay inside these ranges and needn't reach their ends.
Inputs may be any that keep to these rules, and one draw needn't show every extreme that they name: Each row of lengths sums to 4096: one sequence of 2048 tokens and two of 1024 tokens, in an order that may vary from row to row.
All inputs are finite; a program needn't handle non-finite values.
Results may differ from the reference program's by a relative error of at most 0.02.
Values may be sent and summed in bfloat16 or wider, within the bound.
No kernel may reach another device: no remote copies, remote signals or barrier semaphores. Data moves between devices by JAX's collectives and lax.ppermute only.
A program may use at most 192 MiB of HBM per device.

```python
import jax
import jax.numpy as jnp
from jax import lax

D = 1024
HEADS = 16
HEAD_DIM = 64
FF = 4096
SEQS = 3
TOK_X = 4096
TOKENS = 32768
N_GX = 8


def draw_lengths(key, part):
    key = jax.random.fold_in(key, 11)
    longest_at = jax.random.randint(key, (N_GX,), 0, SEQS)
    slots = jnp.arange(SEQS, dtype=jnp.int32)
    return jnp.where(slots[None, :] == longest_at[:, None], TOK_X // 2, TOK_X // 4).astype(jnp.int32)


def block_scale(key, extent, pieces, least, largest):
    loudness, own = 1.0, jax.random.fold_in(key, 6)
    for position, parts in pieces:
        draws = jnp.exp(jax.random.uniform(jax.random.fold_in(own, position), (parts,), jnp.float32, least / len(pieces), largest / len(pieces)))
        loudness = loudness * jnp.repeat(draws, extent[position] // parts).reshape([-1 if axis == position else 1 for axis in range(len(extent))])
    return loudness


def normal_values(rng, extent, width, bound, pieces=(), held_as=jnp.bfloat16):
    level = block_scale(rng, extent, pieces, -0.22, 0.18) if pieces else 1.0
    array = jax.random.normal(rng, extent, jnp.float32) * width * level
    return jnp.minimum(jnp.maximum(array, -bound), bound).astype(held_as)


def setup_inputs(seed: int = 0) -> dict:
    splits = jax.random.split(jax.random.key(seed), 16)
    tokens = normal_values(splits[0], (TOKENS, D), 1.0, 6.0, ((0, 128),))
    ln1_gain = jnp.clip(1.0 + 0.1 * jax.random.normal(splits[1], (D,), jnp.float32), 0.5, 1.5)
    ln1_bias = normal_values(splits[2], (D,), 0.3, 1.75, (), jnp.float32)
    w_qkv = normal_values(splits[3], (D, HEADS, 3 * HEAD_DIM), D ** -0.5, 0.1875, ((0, 8), (1, 16)))
    b_qv = normal_values(splits[4], (HEADS, 2 * HEAD_DIM), 0.3, 1.75, ((0, 16),), jnp.float32)
    w_out = normal_values(splits[5], (HEADS, HEAD_DIM, D), (D // 64) ** -0.5, 1.5, ((0, 16), (2, 8)))
    b_out = normal_values(splits[6], (D,), 0.3, 1.75, (), jnp.float32)
    ln2_gain = jnp.clip(1.0 + 0.1 * jax.random.normal(splits[7], (D,), jnp.float32), 0.5, 1.5)
    ln2_bias = normal_values(splits[8], (D,), 0.3, 1.75, (), jnp.float32)
    w_fc = normal_values(splits[9], (D, FF), D ** -0.5, 0.1875, ((0, 8), (1, 16)))
    b_fc = normal_values(splits[10], (FF,), 0.5, 3.0, ((0, 16),), jnp.float32)
    w_proj = normal_values(splits[11], (FF, D), (FF // 2) ** -0.5, 0.125, ((0, 16), (1, 8)))
    b_proj = normal_values(splits[12], (D,), 0.3, 1.75, (), jnp.float32)
    lengths = draw_lengths(jax.random.fold_in(splits[15], 71), 0)
    cotangent = normal_values(splits[14], (TOKENS, D), 1.0, 6.0, ((0, 128),))
    return dict(tokens=tokens, ln1_gain=ln1_gain, ln1_bias=ln1_bias, w_qkv=w_qkv, b_qv=b_qv, w_out=w_out, b_out=b_out, ln2_gain=ln2_gain, ln2_bias=ln2_bias, w_fc=w_fc, b_fc=b_fc, w_proj=w_proj, b_proj=b_proj, lengths=lengths, cotangent=cotangent)


EPS = 1e-05
MASKED = -1e+30

@jax.custom_vjp
def low(v):
    return lax.optimization_barrier(v.astype(jnp.bfloat16)).astype(jnp.float32)

@jax.custom_vjp
def low_back(v):
    return v

def low_keep(v):
    return (low(v), None)

def low_pass(kept, grad):
    return (grad,)

def back_keep(v):
    return (v, None)

def back_low(kept, grad):
    return (low(grad),)
low.defvjp(low_keep, low_pass)
low_back.defvjp(back_keep, back_low)

def layer_norm(values, gain, shift):
    centre = values - lax.optimization_barrier(jnp.mean(values, axis=-1, keepdims=True))
    spread = lax.optimization_barrier(jnp.mean(centre * centre, axis=-1, keepdims=True))
    return centre * lax.rsqrt(spread + EPS) * gain + shift

def head_attention(query, key_part, value_part, start_row):
    positions = jnp.arange(TOK_X, dtype=jnp.int32)
    scores = jnp.dot(query, key_part.T, precision=lax.Precision.HIGHEST) * HEAD_DIM ** (-0.5)
    scores = low_back(scores)
    visible = (positions[None, :] <= positions[:, None]) & (positions[None, :] >= start_row[:, None])
    scores = jnp.where(visible, scores, MASKED)
    peak = lax.optimization_barrier(jnp.max(scores, axis=-1, keepdims=True))
    powers = jnp.exp(scores - peak)
    attend = powers / lax.optimization_barrier(jnp.sum(powers, axis=-1, keepdims=True))
    return jnp.dot(low(attend), value_part, precision=lax.Precision.HIGHEST)

def group_attention(qkv_group, start_row):
    heads_first = jnp.transpose(qkv_group, (1, 0, 2))
    one_head = jax.checkpoint(head_attention)
    result = lax.map(lambda item: one_head(item[:, :HEAD_DIM], item[:, HEAD_DIM:2 * HEAD_DIM], item[:, 2 * HEAD_DIM:], start_row), heads_first)
    return jnp.transpose(result, (1, 0, 2))

def reference(tokens, ln1_gain, ln1_bias, w_qkv, b_qv, w_out, b_out, ln2_gain, ln2_bias, w_fc, b_fc, w_proj, b_proj, lengths, cotangent):
    highest = lax.Precision.HIGHEST
    ends = jnp.cumsum(lengths, axis=1).astype(jnp.int32)
    positions = jnp.arange(TOK_X, dtype=jnp.int32)
    starts = lax.optimization_barrier(jnp.max(jnp.where(ends[:, None, :] <= positions[None, :, None], ends[:, None, :], 0), axis=2)).astype(jnp.int32)

    def forward(inputs, gain_one, shift_one, qkv_weight, qv_bias, out_weight, out_bias, gain_two, shift_two, fc_weight, fc_bias, proj_weight, proj_bias):
        normed_one = low(layer_norm(inputs, gain_one, shift_one))
        qkv = jnp.einsum('td,dhe->the', normed_one, qkv_weight, precision=highest)
        blank = jnp.zeros((HEADS, HEAD_DIM), jnp.float32)
        bias_full = jnp.concatenate([qv_bias[:, :HEAD_DIM], blank, qv_bias[:, HEAD_DIM:]], axis=1)
        qkv = low(low_back(qkv + bias_full))
        groups = qkv.reshape(N_GX, TOK_X, HEADS, 3 * HEAD_DIM)
        head_out = lax.map(lambda item: group_attention(item[0], item[1]), (groups, starts))
        head_out = low(low_back(head_out.reshape(TOKENS, HEADS * HEAD_DIM)))
        attn_out = low_back(jnp.dot(head_out, out_weight.reshape(HEADS * HEAD_DIM, D), precision=highest)) + out_bias
        middle = inputs + attn_out
        normed_two = low(layer_norm(middle, gain_two, shift_two))
        pre_act = low_back(jnp.dot(normed_two, fc_weight, precision=highest) + fc_bias)
        activated = low(jax.nn.gelu(pre_act, approximate=True))
        mlp_out = low_back(jnp.dot(activated, proj_weight, precision=highest)) + proj_bias
        return middle + mlp_out
    floats = [item.astype(jnp.float32) for item in (tokens, ln1_gain, ln1_bias, w_qkv, b_qv, w_out, b_out, ln2_gain, ln2_bias, w_fc, b_fc, w_proj, b_proj)]
    result, pullback = jax.vjp(forward, *floats)
    grads = pullback(cotangent.astype(jnp.float32))
    return (result.astype(jnp.bfloat16), grads[0], grads[1], grads[2], grads[3], grads[4], grads[5], grads[6], grads[7], grads[8], grads[9], grads[10], grads[11], grads[12])
```

```python
from functools import partial

import jax
import jax.numpy as jnp
from jax import lax
from jax.experimental import pallas as pl
from jax.experimental.pallas import tpu as pltpu
from jax.sharding import Mesh
from jax.sharding import PartitionSpec as P

EPS = 1e-05
MASKED = -1e30
EVERY = ("zh", "y", "zl", "x", "c")
GROUP = ("zl", "x")
F32 = jnp.float32
BF16 = jnp.bfloat16
TILE = 256
RUN = 1024
HEAD_DIM = 64
TOKEN = (8, 128)


def dot(left, right):
    return jnp.dot(left, right, preferred_element_type=F32)


def dot_nt(left, right):
    return lax.dot_general(left, right, (((1,), (1,)), ((), ())), preferred_element_type=F32)


def dot_tn(left, right):
    return lax.dot_general(left, right, (((0,), (0,)), ((), ())), preferred_element_type=F32)


def turn(values):
    return values.astype(F32).T.astype(BF16)


def norm_parts(values):
    centre = values - jnp.mean(values, axis=-1, keepdims=True)
    inverse = lax.rsqrt(jnp.mean(centre * centre, axis=-1, keepdims=True) + EPS)
    return centre * inverse, inverse


def norm_back(grad, normed, inverse, gain):
    g = grad * gain
    return (
        g - jnp.mean(g, axis=-1, keepdims=True) - normed * jnp.mean(g * normed, axis=-1, keepdims=True)
    ) * inverse


def whole(shape):
    return pl.BlockSpec(shape, lambda *_: (0,) * len(shape))


SCALAR = pl.BlockSpec(memory_space=pltpu.SMEM)


def params(mebibytes):
    return pltpu.CompilerParams(vmem_limit_bytes=mebibytes * 1024 * 1024)


def cost(micros):
    return pl.CostEstimate(flops=micros, bytes_accessed=micros, transcendentals=0)


def columns(blocks):
    return jnp.concatenate([blocks[g] for g in range(blocks.shape[0])], axis=1)


ANY = pl.BlockSpec(memory_space=pl.ANY)
CAME = ((0, 16), (16, 16), (32, 16), (48, 16))
SENT = ((32, 8), (40, 8), (16, 8), (24, 8), (48, 8), (56, 8), (0, 16))
PARTS = tuple((far * 16 + first, size) for far in range(4) for first, size in ((0, 4), (4, 6), (10, 6)))
HALVES = len(PARTS)


def slot(place, g, j, sign):
    x, y, z = j % 4, g % 4, (g // 4) * 2 + j // 4
    far_y, far_z = [lax.rem(sign * (place[i] - at) + 8, 4) for i, at in ((2, y), (3, z))]
    return x * 4 + jnp.where(place[0] == 0, far_z * 16 + y, far_y * 16 + z)


def ring_slot(place, g, j):
    x, y, z = j % 4, g % 4, (g // 4) * 2 + j // 4
    far_x, far_y, far_z = [lax.rem(place[i] - at + 8, 4) for i, at in ((1, x), (2, y), (3, z))]
    return far_x * 4 + jnp.where(place[0] == 0, far_z * 16 + far_y, far_y * 16 + far_z)


def load_blocks(arrays, blocks, sems):
    return [
        pltpu.make_async_copy(array, blocks.at[pl.ds(first, size)], sems.at[i])
        for i, (array, (first, size)) in enumerate(zip(arrays, CAME))
    ]


def load_halves(halves, blocks, sems, rows):
    return [
        pltpu.make_async_copy(half.at[:, rows, :], blocks.at[pl.ds(first, size)], sems.at[i])
        for i, (half, (first, size)) in enumerate(zip(halves, PARTS))
    ]


def store_blocks(arrays, blocks, sems):
    return [
        pltpu.make_async_copy(blocks.at[pl.ds(first, size)], array, sems.at[i])
        for i, (array, (first, size)) in enumerate(zip(arrays, SENT))
    ]


NUM_CAME = len(CAME)
NUM_SENT = len(SENT)


def sent_shapes(rows, lanes):
    return [jax.ShapeDtypeStruct((size, rows, lanes), BF16) for unused, size in SENT]


def qkv_body(place, own, other, gain, shift, *refs):
    came = refs[:NUM_CAME]
    out, token, normed, blocks, sems = refs[NUM_CAME + 2 :]
    step = pl.program_id(0)

    @pl.when(step == 0)
    def first():
        copies = load_blocks(came, blocks, sems)
        for copy in copies:
            copy.start()
        rows = own.shape[0]
        token[...] = jnp.zeros_like(token)
        for ref, at in ((own, place[0]), (other, 1 - place[0])):
            unit, unused = norm_parts(ref[...].astype(F32))
            here = pl.ds(pl.multiple_of(at * rows, rows), rows)
            normed[here, :] = (unit * gain[...] + shift[...]).astype(BF16)
        for copy in copies:
            copy.wait()

    heads, units, span = out.shape
    weight = head_weights(place, blocks, step * heads, heads)
    out[...] = dot_nt(weight, normed[...]).astype(BF16).reshape(heads, units, span)


def head_weights(place, blocks, first, heads):
    return jnp.concatenate(
        [
            jnp.concatenate([blocks[slot(place, g, first + i, 1)] for g in range(8)], axis=1)
            for i in range(heads)
        ],
        axis=0,
    )


def qkv_call(place, own, other, gain, shift, came, *after):
    rows, width = own.shape
    unused, units, part = came[0].shape
    js, heads = 8, 4
    return pl.pallas_call(
        qkv_body,
        grid=(js // heads,),
        in_specs=[
            SCALAR,
            whole((rows, width)),
            whole((rows, width)),
            whole((1, width)),
            whole((1, width)),
        ]
        + [ANY] * (NUM_CAME + 2),
        out_specs=[
            pl.BlockSpec((heads, units, 2 * rows), lambda j: (j, 0, 0)),
            whole(TOKEN),
        ],
        out_shape=[
            jax.ShapeDtypeStruct((js, units, 2 * rows), BF16),
            jax.ShapeDtypeStruct(TOKEN, F32),
        ],
        scratch_shapes=[
            pltpu.VMEM((2 * rows, width), BF16),
            pltpu.VMEM((8 * js, units, part), BF16),
            pltpu.SemaphoreType.DMA((NUM_CAME,)),
        ],
        compiler_params=params(24),
        cost_estimate=cost(1),
        name="qkv",
    )(place, own, other, gain, shift, *came, *after)


def longest_at(lengths):
    one, two, three = [lengths[0, i] for i in range(3)]
    longest = jnp.maximum(jnp.maximum(one, two), three)
    return jnp.where(one == longest, 0, jnp.where(two == longest, 1, 2))


def load_heads(qkv, shift, query, value, key_rows):
    dim = query.shape[1]
    span = qkv.shape[2]
    bias = jnp.broadcast_to(shift[...], (2 * dim, 2 * dim)).T[:, :1]
    for p in range(qkv.shape[0]):
        raw = qkv[p]
        query[p] = (raw[:dim].astype(F32) + bias[:dim]).astype(BF16)
        value[p] = (raw[2 * dim :].astype(F32) + bias[dim:]).astype(BF16)
        key_rows[p * span : (p + 1) * span, :] = turn(raw[dim : 2 * dim])


def attend_body(lengths, qkv, bias, out, logs, query, value, key_rows):
    dim = query.shape[1]
    span = qkv.shape[2]
    per_run = RUN // span
    load_heads(qkv, bias, query, value, key_rows)
    causal = lax.broadcasted_iota(jnp.int32, (TILE, TILE), 0) <= lax.broadcasted_iota(
        jnp.int32, (TILE, TILE), 1
    )
    scale = dim ** (-0.5)

    def tile(b, t, extra):
        place, lane = t * TILE // span, (t * TILE) % span
        p = b * per_run + place
        q = (query[p, :, lane : lane + TILE].astype(F32) * scale).astype(BF16)
        chunks = []
        if extra:
            chunks += [((b - 1) * per_run + i, 0, span) for i in range(per_run)]
        chunks += [(b * per_run + i, 0, span) for i in range(place)]
        if lane:
            chunks.append((p, 0, lane))
        scores = []
        for block, start, size in chunks:
            keys = key_rows[pl.ds(pl.multiple_of(block * span + start, TILE), size), :]
            scores.append(dot(keys, q))
        keys = key_rows[pl.ds(pl.multiple_of(p * span + lane, TILE), TILE), :]
        scores.append(jnp.where(causal, dot(keys, q), MASKED))
        chunks.append((p, lane, TILE))
        peak = scores[0].max(axis=0, keepdims=True)
        for s in scores[1:]:
            peak = jnp.maximum(peak, s.max(axis=0, keepdims=True))
        total = jnp.zeros((1, TILE), F32)
        acc = jnp.zeros((dim, TILE), F32)
        for s, (block, start, size) in zip(scores, chunks):
            powers = jnp.exp(s - peak)
            total = total + powers.sum(axis=0, keepdims=True)
            acc = acc + dot(value[block, :, start : start + size], powers.astype(BF16))
        acc = acc / total
        out[p, :, lane : lane + TILE] = acc.astype(BF16)
        logs[p, :, lane : lane + TILE] = peak + jnp.log(total)

    def run(b, carry):
        more = b == longest_at(lengths) + 1

        @pl.when(more)
        def with_extra():
            for t in range(RUN // TILE):
                tile(b, t, True)

        @pl.when(jnp.logical_not(more))
        def alone():
            for t in range(RUN // TILE):
                tile(b, t, False)

        return carry

    lax.fori_loop(0, qkv.shape[0] // per_run, run, 0)


def attend_call(lengths, qkv, bias):
    ps, units, span = qkv.shape
    dim = units // 3
    shape = (ps, dim, span)
    vmem = pl.BlockSpec(memory_space=pltpu.VMEM)
    return pl.pallas_call(
        attend_body,
        in_specs=[SCALAR, vmem, vmem],
        out_specs=[vmem] * 2,
        out_shape=[
            jax.ShapeDtypeStruct(shape, BF16),
            jax.ShapeDtypeStruct((ps, 1, span), F32),
        ],
        scratch_shapes=[
            pltpu.VMEM(shape, BF16),
            pltpu.VMEM(shape, BF16),
            pltpu.VMEM((ps * span, dim), BF16),
        ],
        compiler_params=params(20),
        cost_estimate=cost(1),
        name="attend",
    )(lengths, qkv, bias)


def attend_back_body(
    lengths, qkv, bias, grad, heads, logs, after, out, sums,
    query, value, key_rows, value_rows, query_rows, grad_rows, dots, query_grad,
):
    dim = query.shape[1]
    ps, span = qkv.shape[0], qkv.shape[2]
    per_run = RUN // span
    scale = dim ** (-0.5)
    load_heads(qkv, bias, query, value, key_rows)
    for p in range(ps):
        rows = slice(p * span, (p + 1) * span)
        value_rows[rows, :] = turn(value[p])
        query_rows[rows, :] = turn(query[p])
        grad_rows[rows, :] = turn(grad[p])
        dots[p] = jnp.sum(grad[p].astype(F32) * heads[p].astype(F32), axis=0, keepdims=True)
        query[p] = (query[p].astype(F32) * scale).astype(BF16)
    query_grad[...] = jnp.zeros_like(query_grad)
    causal = lax.broadcasted_iota(jnp.int32, (TILE, TILE), 0) <= lax.broadcasted_iota(
        jnp.int32, (TILE, TILE), 1
    )

    def tile(b, t, extra):
        place, lane = t * TILE // span, (t * TILE) % span
        p = b * per_run + place
        here = pl.ds(pl.multiple_of(p * span + lane, TILE), TILE)
        keys, values = key_rows[here, :], value_rows[here, :]
        keys_t = qkv[p, dim : 2 * dim, lane : lane + TILE]
        chunks = [(p, lane, TILE, True)]
        if lane + TILE < span:
            chunks.append((p, lane + TILE, span - lane - TILE, False))
        chunks += [(b * per_run + i, 0, span, False) for i in range(place + 1, per_run)]
        if extra:
            chunks += [((b + 1) * per_run + i, 0, span, False) for i in range(per_run)]
        key_grad = jnp.zeros((TILE, dim), F32)
        value_grad = jnp.zeros((TILE, dim), F32)
        for block, start, size, masked in chunks:
            lanes = slice(start, start + size)
            attend = jnp.exp(dot(keys, query[block, :, lanes]) - logs[block, :, lanes])
            if masked:
                attend = jnp.where(causal, attend, 0.0)
            attend_grad = dot(values, grad[block, :, lanes])
            score_grad = (attend * (attend_grad - dots[block, :, lanes])).astype(BF16)
            rows = pl.ds(pl.multiple_of(block * span + start, TILE), size)
            query_grad[block, :, lanes] += dot(keys_t, score_grad)
            key_grad = key_grad + dot(score_grad, query_rows[rows, :])
            value_grad = value_grad + dot(attend.astype(BF16), grad_rows[rows, :])
        out[p, dim : 2 * dim, lane : lane + TILE] = turn(key_grad * scale)
        out[p, 2 * dim :, lane : lane + TILE] = turn(value_grad)

    def run(b, carry):
        more = b == longest_at(lengths)

        @pl.when(more)
        def with_extra():
            for t in range(RUN // TILE):
                tile(b, t, True)

        @pl.when(jnp.logical_not(more))
        def alone():
            for t in range(RUN // TILE):
                tile(b, t, False)

        return carry

    lax.fori_loop(0, ps // per_run, run, 0)
    query_sum = jnp.zeros((dim, span), F32)
    value_sum = jnp.zeros((dim, span), F32)
    for p in range(ps):
        low = (query_grad[p] * scale).astype(BF16)
        out[p, :dim, :] = low
        query_sum = query_sum + low.astype(F32)
        value_sum = value_sum + out[p, 2 * dim :, :].astype(F32)
    both = jnp.concatenate([query_sum, value_sum], axis=0)
    both = jnp.broadcast_to(jnp.sum(both, axis=1, keepdims=True), (2 * dim, 2 * dim))
    sums[...] = both.T[:1]


def attend_back_call(lengths, qkv, bias, grad, heads, logs, after):
    ps, units, span = qkv.shape
    dim = units // 3
    shape = (ps, dim, span)
    rows = (ps * span, dim)
    vmem = pl.BlockSpec(memory_space=pltpu.VMEM)
    return pl.pallas_call(
        attend_back_body,
        in_specs=[SCALAR] + [vmem] * 5 + [ANY],
        out_specs=[vmem] * 2,
        out_shape=[
            jax.ShapeDtypeStruct((ps, units, span), BF16),
            jax.ShapeDtypeStruct((1, 2 * dim), F32),
        ],
        scratch_shapes=[
            pltpu.VMEM(shape, BF16),
            pltpu.VMEM(shape, BF16),
            pltpu.VMEM(rows, BF16),
            pltpu.VMEM(rows, BF16),
            pltpu.VMEM(rows, BF16),
            pltpu.VMEM(rows, BF16),
            pltpu.VMEM((ps, 1, span), F32),
            pltpu.VMEM(shape, F32),
        ],
        compiler_params=params(32),
        cost_estimate=cost(1),
        name="attend_back",
    )(lengths, qkv, bias, grad, heads, logs, after)


def out_body(place, heads, *refs):
    halves = refs[:HALVES]
    out, weight, blocks, sems = refs[HALVES:]
    dim, part = blocks.shape[1:]
    copies = load_halves(halves, blocks, sems, pl.ds(halves[0].shape[1] - dim, dim))
    for copy in copies:
        copy.start()
    flat = heads[...].reshape(heads.shape[0] * dim, heads.shape[2])
    for copy in copies:
        copy.wait()
    for j in range(8):
        for g in range(8):
            weight[j * dim : (j + 1) * dim, g * part : (g + 1) * part] = blocks[ring_slot(place, g, j)]
    out[...] = dot_tn(flat, weight[...]).astype(BF16)


def out_call(place, heads, halves):
    js, dim, rows = heads.shape
    part = halves[0].shape[2]
    width = 8 * part
    vmem = pl.BlockSpec(memory_space=pltpu.VMEM)
    return pl.pallas_call(
        out_body,
        in_specs=[SCALAR, vmem] + [ANY] * HALVES,
        out_specs=[vmem] * 2,
        out_shape=[
            jax.ShapeDtypeStruct((rows, width), BF16),
            jax.ShapeDtypeStruct((js * dim, width), BF16),
        ],
        scratch_shapes=[
            pltpu.VMEM((8 * js, dim, part), BF16),
            pltpu.SemaphoreType.DMA((HALVES,)),
        ],
        compiler_params=params(16),
        cost_estimate=cost(1),
        name="out",
    )(place, heads, *halves)


COLUMNS = 2


def feed_body(
    place, own, other, mine, theirs, out_shift, gain, shift, cot_own, cot_other, proj_shift, *refs
):
    halves = refs[:HALVES]
    base, share, grad_share, middle = refs[HALVES : HALVES + 4]
    grads = refs[HALVES + 4 : HALVES + 4 + NUM_SENT]
    normed, cot, acc, grad_acc, blocks, grad_blocks, sems = refs[HALVES + 4 + NUM_SENT :]
    step = pl.program_id(0)
    rows = own.shape[0]
    width = own.shape[1]
    part = blocks.shape[2]
    units = (blocks.shape[1] - EXTRA) // 2
    kept = 2 * units + EXTRA
    c = place[0]
    here = pl.ds(pl.multiple_of(c * rows, rows), rows)
    there = pl.ds(pl.multiple_of((1 - c) * rows, rows), rows)

    @pl.when(step == 0)
    def first():
        copies = load_halves(halves, blocks, sems, pl.ds(0, kept))
        for copy in copies:
            copy.start()
        middle[here, :] = own[...].astype(F32)
        middle[there, :] = other[...].astype(F32)
        cot[here, :] = cot_own[...]
        cot[there, :] = cot_other[...]
        values = middle[...] + (mine[...].astype(F32) + theirs[...].astype(F32)) + out_shift[...]
        middle[...] = values
        unit, unused = norm_parts(values)
        low = (unit * gain[...] + shift[...]).astype(BF16)
        normed[...] = low
        acc[...] = jnp.zeros_like(acc)
        grad_acc[...] = jnp.zeros_like(grad_acc)
        for copy in copies:
            copy.wait()

    pairs = [(step * COLUMNS + i, [ring_slot(place, g, step * COLUMNS + i) for g in range(8)]) for i in range(COLUMNS)]

    def rows_of(first):
        return jnp.concatenate(
            [
                jnp.concatenate([blocks[i, first : first + units, :] for i in spots], axis=1)
                for unused, spots in pairs
            ],
            axis=0,
        )

    fc, proj = rows_of(0), rows_of(units)
    lines = []
    for unused, spots in pairs:
        halves_of = blocks[spots[0], 2 * units : kept, :].astype(F32)
        for i in range(units // part):
            line = halves_of[3 * i : 3 * i + 1] + halves_of[3 * i + 1 : 3 * i + 2] + halves_of[3 * i + 2 : 3 * i + 3]
            lines.append(jnp.broadcast_to(line, (part, part)).T[:, :1])
    pre = dot_nt(fc, normed[...]) + jnp.concatenate(lines, axis=0)
    act_grad = dot_nt(proj, cot[...])
    root = 0.7978845608028654
    square = pre * pre
    bend = jnp.tanh(root * pre * (1.0 + 0.044715 * square))
    half = 0.5 * (1.0 + bend)
    activated = (pre * half).astype(BF16)
    slope = half + 0.5 * pre * (1.0 - bend * bend) * (root * (1.0 + 3 * 0.044715 * square))
    pre_grad = (act_grad * slope).astype(BF16)
    shift_grad = jnp.sum(pre_grad.astype(F32), axis=1, keepdims=True)
    acc[...] += dot_tn(activated, proj)
    grad_acc[...] += dot_tn(pre_grad, fc)
    fc_grad = dot(pre_grad, normed[...]).astype(BF16)
    proj_grad = dot(activated, cot[...]).astype(BF16)
    for n, (j, unused) in enumerate(pairs):
        mine_rows = slice(n * units, (n + 1) * units)
        extra = stack_halves(
            [
                jnp.broadcast_to(shift_grad[n * units + i * part : n * units + (i + 1) * part], (part, part)).T[:1]
                for i in range(units // part)
            ]
        )
        for g in range(8):
            i = slot(place, g, j, -1)
            lanes = slice(g * part, (g + 1) * part)
            grad_blocks[i, :units, :] = fc_grad[mine_rows, lanes]
            grad_blocks[i, units : 2 * units, :] = proj_grad[mine_rows, lanes]
            grad_blocks[i, 2 * units :, :] = extra

    @pl.when(step == pl.num_programs(0) - 1)
    def last():
        copies = store_blocks(grads, grad_blocks, sems)
        for copy in copies:
            copy.start()
        base[...] = middle[here, :] + acc[here, :] + proj_shift[...]
        share[...] = acc[there, :].astype(BF16)
        grad_share[...] = grad_acc[...].astype(BF16)
        for copy in copies:
            copy.wait()


def feed_call(place, own, other, mine, theirs, out_shift, gain, shift, cot_own, cot_other, proj_shift, halves):
    rows, width = own.shape
    unused, packed_rows, part = halves[0].shape
    kept = packed_rows - HEAD_DIM
    row = whole((1, width))
    some, all_rows = whole((rows, width)), whole((2 * rows, width))
    both = (2 * rows, width)
    return pl.pallas_call(
        feed_body,
        grid=(8 // COLUMNS,),
        in_specs=[SCALAR, some, some, all_rows, all_rows, row, row, row, some, some, row] + [ANY] * HALVES,
        out_specs=[some, some, all_rows, all_rows] + [ANY] * NUM_SENT,
        out_shape=[
            jax.ShapeDtypeStruct((rows, width), F32),
            jax.ShapeDtypeStruct((rows, width), BF16),
            jax.ShapeDtypeStruct(both, BF16),
            jax.ShapeDtypeStruct(both, F32),
        ]
        + sent_shapes(kept, part),
        scratch_shapes=[
            pltpu.VMEM(both, BF16),
            pltpu.VMEM(both, BF16),
            pltpu.VMEM(both, F32),
            pltpu.VMEM(both, F32),
            pltpu.VMEM((64, kept, part), BF16),
            pltpu.VMEM((64, kept, part), BF16),
            pltpu.SemaphoreType.DMA((HALVES,)),
        ],
        compiler_params=params(56),
        cost_estimate=cost(1),
        name="feed",
    )(place, own, other, mine, theirs, out_shift, gain, shift, cot_own, cot_other, proj_shift, *halves)


EXTRA = 16


def stack_halves(rows):
    place = lax.broadcasted_iota(jnp.int32, (EXTRA, rows[0].shape[1]), 0)
    block = jnp.zeros(place.shape, F32)
    for i, row in enumerate(rows):
        high = row.astype(BF16).astype(F32)
        block = jnp.where(place == 2 * i, high, block)
        block = jnp.where(place == 2 * i + 1, row - high, block)
    return block.astype(BF16)


def middle_body(
    place, middle, mine, theirs, gain, cot_own, cot_other, heads, weight,
    grad_own, out_grad, sums, weight_grad, cot, scaled,
):
    rows = cot_own.shape[0]
    c = place[0]
    here = pl.ds(pl.multiple_of(c * rows, rows), rows)
    there = pl.ds(pl.multiple_of((1 - c) * rows, rows), rows)
    cot[here, :] = cot_own[...].astype(F32)
    cot[there, :] = cot_other[...].astype(F32)
    unit, inverse = norm_parts(middle[...])
    grad = mine[...].astype(F32) + theirs[...].astype(F32)
    total = cot[...] + norm_back(grad, unit, inverse, gain[...])
    low = total.astype(BF16)
    cot[...] = total
    scaled[...] = grad * unit
    js, dim, span = heads.shape
    out_grad[...] = dot_nt(weight[...], low).astype(BF16).reshape(js, dim, span)
    weight_grad[...] = dot(heads[...].reshape(js * dim, span), low).astype(BF16).reshape(weight_grad.shape)
    kept = cot[here, :]
    grad_own[...] = kept
    sums[0:1, :] = jnp.sum(scaled[here, :], axis=0, keepdims=True)
    scaled[...] = grad
    sums[1:2, :] = jnp.sum(scaled[here, :], axis=0, keepdims=True)
    sums[2:3, :] = jnp.sum(kept, axis=0, keepdims=True)
    sums[3:4, :] = jnp.sum(cot_own[...].astype(F32), axis=0, keepdims=True)


def middle_call(place, middle, mine, theirs, gain, cot_own, cot_other, heads, weight):
    rows, width = cot_own.shape
    js, dim, span = heads.shape
    vmem = pl.BlockSpec(memory_space=pltpu.VMEM)
    return pl.pallas_call(
        middle_body,
        in_specs=[SCALAR] + [vmem] * 8,
        out_specs=[vmem] * 4,
        out_shape=[
            jax.ShapeDtypeStruct((rows, width), F32),
            jax.ShapeDtypeStruct(heads.shape, BF16),
            jax.ShapeDtypeStruct((4, width), F32),
            jax.ShapeDtypeStruct((js, dim, width), BF16),
        ],
        scratch_shapes=[pltpu.VMEM((2 * rows, width), F32)] * 2,
        compiler_params=params(56),
        cost_estimate=cost(1),
        name="middle",
    )(place, middle, mine, theirs, gain, cot_own, cot_other, heads, weight)


def qkv_back_body(place, grad, gain, shift, tokens_own, tokens_other, head_sums, early, out_grad, *refs):
    came = refs[:NUM_CAME]
    own, share, sums = refs[NUM_CAME + 1 : NUM_CAME + 4]
    grads = refs[NUM_CAME + 4 : NUM_CAME + 4 + NUM_SENT]
    acc, unit, normed, blocks, grad_blocks, load_sems, sems = refs[NUM_CAME + 4 + NUM_SENT :]
    step = pl.program_id(0)
    units, part = blocks.shape[1:]
    rows = own.shape[0]
    heads, unused, span = grad.shape
    dim = out_grad.shape[1]
    c = place[0]
    here = pl.ds(pl.multiple_of(c * rows, rows), rows)
    there = pl.ds(pl.multiple_of((1 - c) * rows, rows), rows)

    @pl.when(step == 0)
    def first():
        copies = load_blocks(came, blocks, load_sems)
        for copy in copies:
            copy.start()
        acc[...] = jnp.zeros_like(acc)
        unit[here, :], unused = norm_parts(tokens_own[...].astype(F32))
        unit[there, :], unused = norm_parts(tokens_other[...].astype(F32))
        normed[...] = (unit[...] * gain[...] + shift[...]).astype(BF16)
        for copy in copies:
            copy.wait()

    flat = grad[...].reshape(heads * units, span)
    product = dot(flat, normed[...]).astype(BF16)
    group = lax.rem(place[3], 2) * 4 + place[1]
    for n in range(heads):
        j = step * heads + n
        extra = stack_halves([jnp.where(group == j, head_sums[...], 0.0)])
        for g in range(8):
            i = slot(place, g, j, -1)
            lanes = slice(g * part, (g + 1) * part)
            grad_blocks[i, :units, :] = product[n * units : (n + 1) * units, lanes]
            grad_blocks[i, units : units + dim, :] = out_grad[n, :, lanes]
            grad_blocks[i, units + dim :, :] = extra

    @pl.when(step == pl.num_programs(0) - 1)
    def start_stores():
        for copy in store_blocks(grads, grad_blocks, sems):
            copy.start()

    acc[...] += dot_tn(flat, head_weights(place, blocks, step * heads, heads))

    @pl.when(step == pl.num_programs(0) - 1)
    def last():
        own[...] = acc[here, :]
        share[:rows, :] = acc[there, :].astype(BF16)
        sums[0:4, :] = early[...]
        sums[4:5, :] = jnp.sum(acc[...] * unit[...], axis=0, keepdims=True)
        sums[5:6, :] = jnp.sum(acc[...], axis=0, keepdims=True)
        sums[6:8, :] = jnp.zeros((2, sums.shape[1]), F32)
        share[rows:, :] = stack_halves([sums[i : i + 1, :] for i in range(6)])
        for copy in store_blocks(grads, grad_blocks, sems):
            copy.wait()


def qkv_back_call(place, grad, gain, shift, tokens_own, tokens_other, head_sums, early, out_grad, came, after):
    js, units, both = grad.shape
    part = came[0].shape[2]
    rows, width = tokens_own.shape
    heads = 4
    packed_rows = units + out_grad.shape[1] + EXTRA
    some = whole((rows, width))
    return pl.pallas_call(
        qkv_back_body,
        grid=(js // heads,),
        in_specs=[
            SCALAR,
            pl.BlockSpec((heads, units, both), lambda j: (j, 0, 0)),
            whole((1, width)),
            whole((1, width)),
            some,
            some,
            whole(head_sums.shape),
            whole(early.shape),
            pl.BlockSpec((heads,) + out_grad.shape[1:], lambda j: (j, 0, 0)),
        ]
        + [ANY] * (NUM_CAME + 1),
        out_specs=[some, whole((rows + EXTRA, width)), whole((8, width))] + [ANY] * NUM_SENT,
        out_shape=[
            jax.ShapeDtypeStruct((rows, width), F32),
            jax.ShapeDtypeStruct((rows + EXTRA, width), BF16),
            jax.ShapeDtypeStruct((8, width), F32),
        ]
        + sent_shapes(packed_rows, part),
        scratch_shapes=[
            pltpu.VMEM((both, width), F32),
            pltpu.VMEM((both, width), F32),
            pltpu.VMEM((both, width), BF16),
            pltpu.VMEM((64, units, part), BF16),
            pltpu.VMEM((64, packed_rows, part), BF16),
            pltpu.SemaphoreType.DMA((NUM_CAME,)),
            pltpu.SemaphoreType.DMA((NUM_SENT,)),
        ],
        compiler_params=params(56),
        cost_estimate=cost(1),
        name="qkv_back",
    )(place, grad, gain, shift, tokens_own, tokens_other, head_sums, early, out_grad, *came, after)


def input_body(own, share, sums, inputs, gain, middle_grad, out, total):
    rows = own.shape[0]
    unit, inverse = norm_parts(inputs[...].astype(F32))
    grad = own[...] + share[:rows, :].astype(F32)
    out[...] = middle_grad[...] + norm_back(grad, unit, inverse, gain[...])
    halves = share[rows:, :].astype(F32)
    for i in range(sums.shape[0]):
        total[i : i + 1, :] = sums[i : i + 1, :] + (halves[2 * i : 2 * i + 1] + halves[2 * i + 1 : 2 * i + 2])


def input_call(own, share, sums, inputs, gain, middle_grad):
    rows, width = own.shape
    vmem = pl.BlockSpec(memory_space=pltpu.VMEM)
    return pl.pallas_call(
        input_body,
        in_specs=[vmem] * 6,
        out_specs=[vmem] * 2,
        out_shape=[jax.ShapeDtypeStruct((rows, width), F32), jax.ShapeDtypeStruct(sums.shape, F32)],
        compiler_params=params(12),
        cost_estimate=cost(1),
        name="input",
    )(own, share, sums, inputs, gain, middle_grad)


def pack_body(w_qkv, w_fc, w_proj, w_out, shift, spread, feed):
    for i in range(spread.shape[0]):
        spread[i] = w_qkv[...]
    units, part = w_proj.shape
    feed[:units, :] = turn(w_fc[...])
    feed[units : 2 * units, :] = w_proj[...]
    place = lax.broadcasted_iota(jnp.int32, (EXTRA, part), 0)
    block = jnp.zeros(place.shape, F32)
    for n in range(units // part):
        rest = shift[:, n * part : (n + 1) * part]
        for i in range(3):
            high = rest.astype(BF16).astype(F32)
            block = jnp.where(place == 3 * n + i, high, block)
            rest = rest - high
    feed[2 * units : 2 * units + EXTRA, :] = block.astype(BF16)
    feed[2 * units + EXTRA :, :] = w_out[...]


def pack_call(w_qkv, w_fc, w_proj, w_out, shift):
    units, part = w_proj.shape
    vmem = pl.BlockSpec(memory_space=pltpu.VMEM)
    return pl.pallas_call(
        pack_body,
        in_specs=[vmem] * 5,
        out_specs=[vmem] * 2,
        out_shape=[
            jax.ShapeDtypeStruct((16,) + w_qkv.shape, BF16),
            jax.ShapeDtypeStruct((2 * units + EXTRA + w_out.shape[0], part), BF16),
        ],
        compiler_params=params(56),
        cost_estimate=cost(1),
        name="pack",
    )(w_qkv, w_fc, w_proj, w_out, shift)


def join_body(groups, *refs):
    ins, outs, sems = refs[: -len(groups) - 2], refs[-len(groups) - 1 : -1], refs[-1]
    copies = []
    for out, group in zip(outs, groups):
        at = 0
        for i, first, size in group:
            source = ins[i] if first is None else ins[i].at[pl.ds(first, size)]
            target = out.at[at] if first is None else out.at[pl.ds(at, size)]
            copies.append(pltpu.make_async_copy(source, target, sems.at[len(copies)]))
            at += size
    for copy in copies:
        copy.start()
    for copy in copies:
        copy.wait()


def join_call(arrays, groups, after):
    shape = arrays[0].shape if groups[0][0][1] is None else arrays[0].shape[1:]
    return pl.pallas_call(
        partial(join_body, groups),
        in_specs=[ANY] * (len(arrays) + 1),
        out_specs=[pl.BlockSpec(memory_space=pltpu.VMEM)] * len(groups),
        out_shape=[
            jax.ShapeDtypeStruct((sum(size for unused, unused_too, size in group),) + shape, BF16)
            for group in groups
        ],
        scratch_shapes=[pltpu.SemaphoreType.DMA((sum(len(group) for group in groups),))],
        compiler_params=params(6),
        cost_estimate=cost(1),
        name="join",
    )(*arrays, after)


def relay_body(left_low, right_high, from_left, from_right, after, sent_low, sent_high, token):
    token[...] = jnp.zeros_like(token)
    sent_low[...] = (left_low[...].astype(F32) + from_left[...].astype(F32)).astype(BF16)
    sent_high[...] = (right_high[...].astype(F32) + from_right[...].astype(F32)).astype(BF16)


def relay_call(left_low, right_high, from_left, from_right, after, mebibytes):
    vmem = pl.BlockSpec(memory_space=pltpu.VMEM)
    return pl.pallas_call(
        relay_body,
        in_specs=[vmem] * 4 + [ANY],
        out_specs=[vmem] * 3,
        out_shape=[jax.ShapeDtypeStruct(left_low.shape, BF16)] * 2 + [jax.ShapeDtypeStruct(TOKEN, F32)],
        compiler_params=params(mebibytes),
        cost_estimate=cost(1),
        name="relay",
    )(left_low, right_high, from_left, from_right, after)


def total_body(place, stays, got_low, got_high, more_low, more_high, after, *outs):
    at = jnp.where(place[0] == 0, place[2], place[3])
    for shift, out in enumerate(outs):
        w = lax.rem(at + shift, 4)
        for x in range(4):
            got, more = (got_low, more_low) if x < 2 else (got_high, more_high)
            i = x % 2 * 4 + w
            total = stays[x * 4 + w].astype(F32) + got[i].astype(F32) + more[i].astype(F32)
            out[x] = total.astype(BF16)


def total_call(place, stays, got_low, got_high, more_low, more_high, after):
    vmem = pl.BlockSpec(memory_space=pltpu.VMEM)
    return pl.pallas_call(
        total_body,
        in_specs=[SCALAR] + [vmem] * 5 + [ANY],
        out_specs=[vmem] * 4,
        out_shape=[jax.ShapeDtypeStruct((4,) + stays.shape[1:], BF16)] * 4,
        compiler_params=params(20),
        cost_estimate=cost(1),
        name="total",
    )(place, stays, got_low, got_high, more_low, more_high, after)


def next_body(place, one, two, three, four, *refs):
    outs, token = refs[:4], refs[4]
    token[...] = jnp.zeros_like(token)
    for shift, out in enumerate(outs):
        x = lax.rem(place[1] + shift, 4)
        total = one[x].astype(F32) + two[x].astype(F32) + three[x].astype(F32) + four[x].astype(F32)
        out[...] = total.astype(BF16)


def next_call(place, arrays):
    vmem = pl.BlockSpec(memory_space=pltpu.VMEM)
    shape = arrays[0].shape[1:]
    return pl.pallas_call(
        next_body,
        in_specs=[SCALAR] + [vmem] * 4,
        out_specs=[vmem] * 5,
        out_shape=[jax.ShapeDtypeStruct(shape, BF16)] * 4 + [jax.ShapeDtypeStruct(TOKEN, F32)],
        compiler_params=params(16),
        cost_estimate=cost(1),
        name="next",
    )(place, *arrays)


VECTORS = 6


def total_last_body(stays, got_low, got_high, more_low, more_high, one, two, three, four, after, out):
    size, rows, lanes = stays.shape
    vectors = (one[...] + two[...]) + (three[...] + four[...])
    wide = vectors.shape[1] // lanes
    count = VECTORS * wide
    place = lax.broadcasted_iota(jnp.int32, (2 * count, lanes), 0)
    block = jnp.zeros(place.shape, F32)
    for v in range(VECTORS):
        for k in range(wide):
            row = vectors[v : v + 1, k * lanes : (k + 1) * lanes]
            high = row.astype(BF16).astype(F32)
            block = jnp.where(place == v * wide + k, high, block)
            block = jnp.where(place == count + v * wide + k, row - high, block)
    block = block.astype(BF16)
    for i in range(size):
        got, more = (got_low, more_low) if i < size // 2 else (got_high, more_high)
        k = i % (size // 2)
        out[i, :rows, :] = (stays[i].astype(F32) + got[k].astype(F32) + more[k].astype(F32)).astype(BF16)
        out[i, rows:, :] = block


def total_last_call(stays, got_low, got_high, more_low, more_high, terms, after):
    size, rows, lanes = stays.shape
    more = 2 * VECTORS * terms[0].shape[1] // lanes
    vmem = pl.BlockSpec(memory_space=pltpu.VMEM)
    return pl.pallas_call(
        total_last_body,
        in_specs=[vmem] * 9 + [ANY],
        out_specs=vmem,
        out_shape=jax.ShapeDtypeStruct((size, rows + more, lanes), BF16),
        compiler_params=params(56),
        cost_estimate=cost(1),
        name="total_last",
    )(stays, got_low, got_high, more_low, more_high, *terms, after)


def gate_body(*refs):
    pass


def gate(arrays, after, mebibytes=1):
    return pl.pallas_call(
        gate_body,
        in_specs=[ANY] * (len(arrays) + 1),
        out_specs=[ANY] * len(arrays),
        out_shape=[jax.ShapeDtypeStruct(array.shape, array.dtype) for array in arrays],
        input_output_aliases={i: i for i in range(len(arrays))},
        compiler_params=params(mebibytes),
        cost_estimate=cost(1),
        name="gate",
    )(*arrays, after)


def sum_blocks(blocks):
    values = blocks[0].astype(F32)
    for i in range(1, blocks.shape[0]):
        values = values + blocks[i].astype(F32)
    return values


def feed_end_body(one, two, three, four, fc, proj, shift):
    total = one[...].astype(F32) + two[...].astype(F32) + three[...].astype(F32) + four[...].astype(F32)
    units, part = proj.shape
    fc[...] = total[:units].T
    proj[...] = total[units : 2 * units]
    for i in range(units // part):
        first = 2 * units + 2 * i
        shift[:, i * part : (i + 1) * part] = total[first : first + 1] + total[first + 1 : first + 2]


def feed_end_call(arrays, units):
    part = arrays[0].shape[1]
    vmem = pl.BlockSpec(memory_space=pltpu.VMEM)
    return pl.pallas_call(
        feed_end_body,
        in_specs=[vmem] * 4,
        out_specs=[vmem] * 3,
        out_shape=[
            jax.ShapeDtypeStruct((part, units), F32),
            jax.ShapeDtypeStruct((units, part), F32),
            jax.ShapeDtypeStruct((1, units), F32),
        ],
        compiler_params=params(12),
        cost_estimate=cost(1),
        name="feed_end",
    )(*arrays)


def qkv_end_body(blocks, weight, out, shift, *vectors):
    total = sum_blocks(blocks)
    units, part = weight.shape
    dim = out.shape[0]
    weight[...] = total[:units]
    out[...] = total[units : units + dim]
    kept = units + dim
    shift[...] = total[kept : kept + 1] + total[kept + 1 : kept + 2]
    wide = vectors[0].shape[1] // part
    count = VECTORS * wide
    first = kept + EXTRA
    for v in range(VECTORS):
        for k in range(wide):
            i = first + v * wide + k
            vectors[v][:, k * part : (k + 1) * part] = total[i : i + 1] + total[i + count : i + count + 1]


def qkv_end_call(blocks, dim, width):
    unused, rows, part = blocks.shape
    vmem = pl.BlockSpec(memory_space=pltpu.VMEM)
    return pl.pallas_call(
        qkv_end_body,
        in_specs=[vmem],
        out_specs=[vmem] * (3 + VECTORS),
        out_shape=[
            jax.ShapeDtypeStruct((rows - dim - EXTRA - 2 * VECTORS * width // part, part), F32),
            jax.ShapeDtypeStruct((dim, part), F32),
            jax.ShapeDtypeStruct((1, part), F32),
        ]
        + [jax.ShapeDtypeStruct((1, width), F32)] * VECTORS,
        compiler_params=params(12),
        cost_estimate=cost(1),
        name="qkv_end",
    )(blocks)


def swap(values):
    return lax.ppermute(values, "c", [(0, 1), (1, 0)])


def trade(values, names):
    return lax.all_to_all(values, names, 0, 0, tiled=True)


def device(x, y, z, c):
    return (((z // 2 * 4 + y) * 2 + z % 2) * 4 + x) * 2 + c


PLANES = [[device(x, y, z, 0) for x in range(4) for y in range(4)] for z in range(4)] + [
    [device(x, y, z, 1) for x in range(4) for z in range(4)] for y in range(4)
]


def trade_plane(values):
    return lax.all_to_all(values, EVERY, 0, 0, axis_index_groups=PLANES, tiled=True)


def move(values, shift, axes="zy"):
    pairs = []
    for x in range(4):
        for y in range(4):
            for z in range(4):
                for c in range(2):
                    to = {"x": x, "y": y, "z": z}
                    to[axes[c]] = (to[axes[c]] + shift) % 4
                    pairs.append((device(x, y, z, c), device(c=c, **to)))
    return lax.ppermute(values, EVERY, sorted(pairs))


def gather_ring(values, axes):
    return [values] + [move(values, shift, axes) for shift in (1, 2, 3)]


def on_device(
    tokens, ln1_gain, ln1_bias, w_qkv, b_qv, w_out, b_out, ln2_gain, ln2_bias,
    w_fc, b_fc, w_proj, b_proj, lengths, cotangent,
):
    place = jnp.stack(
        [
            lax.axis_index("c"),
            lax.axis_index("x"),
            lax.axis_index("y"),
            lax.axis_index("zh") * 2 + lax.axis_index("zl"),
        ]
    ).astype(jnp.int32)
    line = lambda vector: vector.reshape(1, -1)

    tokens_other = swap(tokens)
    cot_other = swap(cotangent)

    spread, feed_shard = pack_call(
        jnp.transpose(w_qkv, (1, 2, 0))[0], w_fc, w_proj, w_out[0], line(b_fc)
    )
    qkv_plane = trade_plane(spread)
    ones = gather_ring(feed_shard, "yz")
    one = join_call(ones, (tuple((i, None, 1) for i in range(4)),), feed_shard)[0]
    qkv_plane = gate([qkv_plane], one)[0]
    left, right, near, last, one_left = gate(
        [move(qkv_plane, 1), move(qkv_plane, 3), move(one, 1, "xx"), move(one, 3, "xx"), move(one, 1)], place
    )
    far_left, far, one_right, one_far = gate(
        [move(left, 1), move(near, 1, "xx"), move(one, 3), move(one_left, 1)], place
    )
    qkv_weight = [qkv_plane, left, far_left, right]

    qkv, token = qkv_call(
        place, tokens, tokens_other, line(ln1_gain), line(ln1_bias), qkv_weight, cot_other, far
    )
    low, high = join_call([near, far, last], (((0, 0, 4), (1, 0, 2)), ((1, 2, 2), (2, 0, 4))), token)
    qkv = trade(qkv, GROUP)
    low_left, high_right, high_left, low_right = move(low, 1), move(high, 3), move(high, 1), move(low, 3)
    heads, logs = attend_call(lengths, qkv, b_qv)
    head_out = heads
    low_left, high_right = gate([low_left, high_right], logs)
    feed_weight = [one, low, high, one_left, low_left, high_left]
    feed_weight += [one_far, move(low_left, 1), move(high_right, 3), one_right, low_right, high_right]
    heads = trade(heads, GROUP)
    mine, out_weight = out_call(place, heads, feed_weight)
    theirs = swap(mine)
    base, share, grad_mine, middle, *feed_grad = feed_call(
        place, tokens, tokens_other, mine, theirs, line(b_out), line(ln2_gain), line(ln2_bias),
        cotangent, cot_other, line(b_proj), feed_weight,
    )
    activations = (base + swap(share).astype(F32)).astype(BF16)
    grad_theirs = swap(grad_mine)
    far_low, far_high, left_low, left_high, right_low, right_high, stays = feed_grad
    from_left, from_right = move(far_low, 1), move(far_high, 3)
    middle_grad, out_grad, sums, out_weight_grad = middle_call(
        place, middle, grad_mine, grad_theirs, line(ln2_gain), cotangent, cot_other, heads, out_weight
    )
    sent_low, sent_high, token = relay_call(left_low, right_high, from_left, from_right, sums, 56)
    out_grad = trade(out_grad, GROUP)
    sent_low, sent_high = gate([sent_low, sent_high], out_grad)
    qkv_grad, head_sums = attend_back_call(lengths, qkv, b_qv, out_grad, head_out, logs, sent_low)
    got_high, got_low, more_low, more_high = gate(
        [move(left_high, 1), move(right_low, 3), move(sent_low, 1), move(sent_high, 3)], head_sums
    )
    qkv_grad = gate([qkv_grad], more_low)[0]
    steps = total_call(place, stays, got_low, got_high, more_low, more_high, head_sums)
    qkv_grad = trade(qkv_grad, GROUP)
    *steps, token = next_call(place, [steps[0]] + [move(steps[shift], shift, "yz") for shift in (1, 2, 3)])
    feed_blocks = [steps[0]] + [move(steps[shift], shift, "xx") for shift in (1, 2, 3)]

    own, share_one, sums, far_low, far_high, left_low, left_high, right_low, right_high, stays = qkv_back_call(
        place, qkv_grad, line(ln1_gain), line(ln1_bias), tokens, tokens_other, head_sums, sums, out_weight_grad,
        qkv_weight, token
    )
    from_left, from_right = move(far_low, 1), move(far_high, 3)
    got_high, got_low = move(left_high, 1), move(right_low, 3)
    sent_low, sent_high, unused = relay_call(left_low, right_high, from_left, from_right, place, 56)
    more_low, more_high = move(sent_low, 1), move(sent_high, 3)
    input_grad, sums = input_call(own, swap(share_one), sums, tokens, line(ln1_gain), middle_grad)
    grad_w_fc, grad_w_proj, grad_b_fc = feed_end_call(feed_blocks, w_fc.shape[1])
    qkv_total = total_last_call(
        stays, got_low, got_high, more_low, more_high, gather_ring(sums, "zy"), grad_b_fc
    )
    qkv_blocks = trade_plane(qkv_total)
    grad_w_qkv, grad_w_out, grad_b_qv, *sums = qkv_end_call(qkv_blocks, w_out.shape[1], tokens.shape[1])
    return (
        activations,
        input_grad,
        sums[4].reshape(-1),
        sums[5].reshape(-1),
        jnp.transpose(grad_w_qkv[None], (2, 0, 1)),
        grad_b_qv,
        grad_w_out.reshape(w_out.shape),
        sums[2].reshape(-1),
        sums[0].reshape(-1),
        sums[1].reshape(-1),
        grad_w_fc,
        grad_b_fc.reshape(-1),
        grad_w_proj,
        sums[3].reshape(-1),
    )


def solution(mesh):
    chips = Mesh(mesh.devices.reshape(2, 4, 2, 4, 2), EVERY)
    gx, gy = ("zh", "y"), ("zl", "x", "c")
    in_specs = (
        P(EVERY, None),
        P(),
        P(),
        P(gx, gy, None),
        P(gy, None),
        P(gy, None, gx),
        P(),
        P(),
        P(),
        P(gx, gy),
        P(gy),
        P(gy, gx),
        P(),
        P(gx, None),
        P(EVERY, None),
    )
    out_specs = (
        P(EVERY, None),
        P(EVERY, None),
        P(),
        P(),
        P(gx, gy, None),
        P(gy, None),
        P(gy, None, gx),
        P(),
        P(),
        P(),
        P(gx, gy),
        P(gy),
        P(gy, gx),
        P(),
    )
    return jax.shard_map(
        on_device, mesh=chips, in_specs=in_specs, out_specs=out_specs, check_vma=False
    )
```

```python
from functools import partial

import jax
import jax.numpy as jnp
from jax import lax
from jax.experimental import pallas as pl
from jax.experimental.pallas import tpu as pltpu
from jax.sharding import Mesh
from jax.sharding import PartitionSpec as P

EPS = 1e-05
MASKED = -1e30
EVERY = ("zh", "y", "zl", "x", "c")
GROUP = ("zl", "x")
F32 = jnp.float32
BF16 = jnp.bfloat16
TILE = 256
RUN = 1024
HEAD_DIM = 64
TOKEN = (8, 128)


def dot(left, right):
    return jnp.dot(left, right, preferred_element_type=F32)


def dot_nt(left, right):
    return lax.dot_general(left, right, (((1,), (1,)), ((), ())), preferred_element_type=F32)


def dot_tn(left, right):
    return lax.dot_general(left, right, (((0,), (0,)), ((), ())), preferred_element_type=F32)


def turn(values):
    return values.astype(F32).T.astype(BF16)


def norm_parts(values):
    centre = values - jnp.mean(values, axis=-1, keepdims=True)
    inverse = lax.rsqrt(jnp.mean(centre * centre, axis=-1, keepdims=True) + EPS)
    return centre * inverse, inverse


def norm_back(grad, normed, inverse, gain):
    g = grad * gain
    return (
        g - jnp.mean(g, axis=-1, keepdims=True) - normed * jnp.mean(g * normed, axis=-1, keepdims=True)
    ) * inverse


def whole(shape):
    return pl.BlockSpec(shape, lambda *_: (0,) * len(shape))


SCALAR = pl.BlockSpec(memory_space=pltpu.SMEM)


def params(mebibytes):
    return pltpu.CompilerParams(vmem_limit_bytes=mebibytes * 1024 * 1024)


def cost(micros):
    return pl.CostEstimate(flops=micros, bytes_accessed=micros, transcendentals=0)


def columns(blocks):
    return jnp.concatenate([blocks[g] for g in range(blocks.shape[0])], axis=1)


ANY = pl.BlockSpec(memory_space=pl.ANY)
CAME = ((0, 16), (16, 16), (32, 16), (48, 16))
SENT = ((32, 8), (40, 8), (16, 8), (24, 8), (48, 8), (56, 8), (0, 16))
PARTS = tuple((far * 16 + first, size) for far in range(4) for first, size in ((0, 4), (4, 6), (10, 6)))
HALVES = len(PARTS)


def slot(place, g, j, sign):
    x, y, z = j % 4, g % 4, (g // 4) * 2 + j // 4
    far_y, far_z = [lax.rem(sign * (place[i] - at) + 8, 4) for i, at in ((2, y), (3, z))]
    return x * 4 + jnp.where(place[0] == 0, far_z * 16 + y, far_y * 16 + z)


def ring_slot(place, g, j):
    x, y, z = j % 4, g % 4, (g // 4) * 2 + j // 4
    far_x, far_y, far_z = [lax.rem(place[i] - at + 8, 4) for i, at in ((1, x), (2, y), (3, z))]
    return far_x * 4 + jnp.where(place[0] == 0, far_z * 16 + far_y, far_y * 16 + far_z)


def load_blocks(arrays, blocks, sems):
    return [
        pltpu.make_async_copy(array, blocks.at[pl.ds(first, size)], sems.at[i])
        for i, (array, (first, size)) in enumerate(zip(arrays, CAME))
    ]


def load_halves(halves, blocks, sems, rows):
    return [
        pltpu.make_async_copy(half.at[:, rows, :], blocks.at[pl.ds(first, size)], sems.at[i])
        for i, (half, (first, size)) in enumerate(zip(halves, PARTS))
    ]


def store_blocks(arrays, blocks, sems):
    return [
        pltpu.make_async_copy(blocks.at[pl.ds(first, size)], array, sems.at[i])
        for i, (array, (first, size)) in enumerate(zip(arrays, SENT))
    ]


NUM_CAME = len(CAME)
NUM_SENT = len(SENT)


def sent_shapes(rows, lanes):
    return [jax.ShapeDtypeStruct((size, rows, lanes), BF16) for unused, size in SENT]


def qkv_body(place, own, other, gain, shift, *refs):
    came = refs[:NUM_CAME]
    out, token, normed, blocks, sems = refs[NUM_CAME + 2 :]
    step = pl.program_id(0)

    @pl.when(step == 0)
    def first():
        copies = load_blocks(came, blocks, sems)
        for copy in copies:
            copy.start()
        rows = own.shape[0]
        token[...] = jnp.zeros_like(token)
        for ref, at in ((own, place[0]), (other, 1 - place[0])):
            unit, unused = norm_parts(ref[...].astype(F32))
            here = pl.ds(pl.multiple_of(at * rows, rows), rows)
            normed[here, :] = (unit * gain[...] + shift[...]).astype(BF16)
        for copy in copies:
            copy.wait()

    heads, units, span = out.shape
    weight = head_weights(place, blocks, step * heads, heads)
    out[...] = dot_nt(weight, normed[...]).astype(BF16).reshape(heads, units, span)


def head_weights(place, blocks, first, heads):
    return jnp.concatenate(
        [
            jnp.concatenate([blocks[slot(place, g, first + i, 1)] for g in range(8)], axis=1)
            for i in range(heads)
        ],
        axis=0,
    )


def qkv_call(place, own, other, gain, shift, came, *after):
    rows, width = own.shape
    unused, units, part = came[0].shape
    js, heads = 8, 4
    return pl.pallas_call(
        qkv_body,
        grid=(js // heads,),
        in_specs=[
            SCALAR,
            whole((rows, width)),
            whole((rows, width)),
            whole((1, width)),
            whole((1, width)),
        ]
        + [ANY] * (NUM_CAME + 2),
        out_specs=[
            pl.BlockSpec((heads, units, 2 * rows), lambda j: (j, 0, 0)),
            whole(TOKEN),
        ],
        out_shape=[
            jax.ShapeDtypeStruct((js, units, 2 * rows), BF16),
            jax.ShapeDtypeStruct(TOKEN, F32),
        ],
        scratch_shapes=[
            pltpu.VMEM((2 * rows, width), BF16),
            pltpu.VMEM((8 * js, units, part), BF16),
            pltpu.SemaphoreType.DMA((NUM_CAME,)),
        ],
        compiler_params=params(24),
        cost_estimate=cost(1),
        name="qkv",
    )(place, own, other, gain, shift, *came, *after)


def longest_at(lengths):
    one, two, three = [lengths[0, i] for i in range(3)]
    longest = jnp.maximum(jnp.maximum(one, two), three)
    return jnp.where(one == longest, 0, jnp.where(two == longest, 1, 2))


def load_heads(qkv, shift, query, value, key_rows):
    dim = query.shape[1]
    span = qkv.shape[2]
    bias = jnp.broadcast_to(shift[...], (2 * dim, 2 * dim)).T[:, :1]
    for p in range(qkv.shape[0]):
        raw = qkv[p]
        query[p] = (raw[:dim].astype(F32) + bias[:dim]).astype(BF16)
        value[p] = (raw[2 * dim :].astype(F32) + bias[dim:]).astype(BF16)
        key_rows[p * span : (p + 1) * span, :] = turn(raw[dim : 2 * dim])


def attend_body(lengths, qkv, bias, out, logs, query, value, key_rows):
    dim = query.shape[1]
    span = qkv.shape[2]
    per_run = RUN // span
    load_heads(qkv, bias, query, value, key_rows)
    causal = lax.broadcasted_iota(jnp.int32, (TILE, TILE), 0) <= lax.broadcasted_iota(
        jnp.int32, (TILE, TILE), 1
    )
    scale = dim ** (-0.5)

    def tile(b, t, extra):
        place, lane = t * TILE // span, (t * TILE) % span
        p = b * per_run + place
        q = (query[p, :, lane : lane + TILE].astype(F32) * scale).astype(BF16)
        chunks = []
        if extra:
            chunks += [((b - 1) * per_run + i, 0, span) for i in range(per_run)]
        chunks += [(b * per_run + i, 0, span) for i in range(place)]
        if lane:
            chunks.append((p, 0, lane))
        scores = []
        for block, start, size in chunks:
            keys = key_rows[pl.ds(pl.multiple_of(block * span + start, TILE), size), :]
            scores.append(dot(keys, q))
        keys = key_rows[pl.ds(pl.multiple_of(p * span + lane, TILE), TILE), :]
        scores.append(jnp.where(causal, dot(keys, q), MASKED))
        chunks.append((p, lane, TILE))
        peak = scores[0].max(axis=0, keepdims=True)
        for s in scores[1:]:
            peak = jnp.maximum(peak, s.max(axis=0, keepdims=True))
        total = jnp.zeros((1, TILE), F32)
        acc = jnp.zeros((dim, TILE), F32)
        for s, (block, start, size) in zip(scores, chunks):
            powers = jnp.exp(s - peak)
            total = total + powers.sum(axis=0, keepdims=True)
            acc = acc + dot(value[block, :, start : start + size], powers.astype(BF16))
        acc = acc / total
        out[p, :, lane : lane + TILE] = acc.astype(BF16)
        logs[p, :, lane : lane + TILE] = peak + jnp.log(total)

    def run(b, carry):
        more = b == longest_at(lengths) + 1

        @pl.when(more)
        def with_extra():
            for t in range(RUN // TILE):
                tile(b, t, True)

        @pl.when(jnp.logical_not(more))
        def alone():
            for t in range(RUN // TILE):
                tile(b, t, False)

        return carry

    lax.fori_loop(0, qkv.shape[0] // per_run, run, 0)


def attend_call(lengths, qkv, bias):
    ps, units, span = qkv.shape
    dim = units // 3
    shape = (ps, dim, span)
    vmem = pl.BlockSpec(memory_space=pltpu.VMEM)
    return pl.pallas_call(
        attend_body,
        in_specs=[SCALAR, vmem, vmem],
        out_specs=[vmem] * 2,
        out_shape=[
            jax.ShapeDtypeStruct(shape, BF16),
            jax.ShapeDtypeStruct((ps, 1, span), F32),
        ],
        scratch_shapes=[
            pltpu.VMEM(shape, BF16),
            pltpu.VMEM(shape, BF16),
            pltpu.VMEM((ps * span, dim), BF16),
        ],
        compiler_params=params(20),
        cost_estimate=cost(1),
        name="attend",
    )(lengths, qkv, bias)


def attend_back_body(
    lengths, qkv, bias, grad, heads, logs, after, out, sums,
    query, value, key_rows, value_rows, query_rows, grad_rows, dots, query_grad,
):
    dim = query.shape[1]
    ps, span = qkv.shape[0], qkv.shape[2]
    per_run = RUN // span
    scale = dim ** (-0.5)
    load_heads(qkv, bias, query, value, key_rows)
    for p in range(ps):
        rows = slice(p * span, (p + 1) * span)
        value_rows[rows, :] = turn(value[p])
        query_rows[rows, :] = turn(query[p])
        grad_rows[rows, :] = turn(grad[p])
        dots[p] = jnp.sum(grad[p].astype(F32) * heads[p].astype(F32), axis=0, keepdims=True)
        query[p] = (query[p].astype(F32) * scale).astype(BF16)
    query_grad[...] = jnp.zeros_like(query_grad)
    causal = lax.broadcasted_iota(jnp.int32, (TILE, TILE), 0) <= lax.broadcasted_iota(
        jnp.int32, (TILE, TILE), 1
    )

    def tile(b, t, extra):
        place, lane = t * TILE // span, (t * TILE) % span
        p = b * per_run + place
        here = pl.ds(pl.multiple_of(p * span + lane, TILE), TILE)
        keys, values = key_rows[here, :], value_rows[here, :]
        keys_t = qkv[p, dim : 2 * dim, lane : lane + TILE]
        chunks = [(p, lane, TILE, True)]
        if lane + TILE < span:
            chunks.append((p, lane + TILE, span - lane - TILE, False))
        chunks += [(b * per_run + i, 0, span, False) for i in range(place + 1, per_run)]
        if extra:
            chunks += [((b + 1) * per_run + i, 0, span, False) for i in range(per_run)]
        key_grad = jnp.zeros((TILE, dim), F32)
        value_grad = jnp.zeros((TILE, dim), F32)
        for block, start, size, masked in chunks:
            lanes = slice(start, start + size)
            attend = jnp.exp(dot(keys, query[block, :, lanes]) - logs[block, :, lanes])
            if masked:
                attend = jnp.where(causal, attend, 0.0)
            attend_grad = dot(values, grad[block, :, lanes])
            score_grad = (attend * (attend_grad - dots[block, :, lanes])).astype(BF16)
            rows = pl.ds(pl.multiple_of(block * span + start, TILE), size)
            query_grad[block, :, lanes] += dot(keys_t, score_grad)
            key_grad = key_grad + dot(score_grad, query_rows[rows, :])
            value_grad = value_grad + dot(attend.astype(BF16), grad_rows[rows, :])
        out[p, dim : 2 * dim, lane : lane + TILE] = turn(key_grad * scale)
        out[p, 2 * dim :, lane : lane + TILE] = turn(value_grad)

    def run(b, carry):
        more = b == longest_at(lengths)

        @pl.when(more)
        def with_extra():
            for t in range(RUN // TILE):
                tile(b, t, True)

        @pl.when(jnp.logical_not(more))
        def alone():
            for t in range(RUN // TILE):
                tile(b, t, False)

        return carry

    lax.fori_loop(0, ps // per_run, run, 0)
    query_sum = jnp.zeros((dim, span), F32)
    value_sum = jnp.zeros((dim, span), F32)
    for p in range(ps):
        low = (query_grad[p] * scale).astype(BF16)
        out[p, :dim, :] = low
        query_sum = query_sum + low.astype(F32)
        value_sum = value_sum + out[p, 2 * dim :, :].astype(F32)
    both = jnp.concatenate([query_sum, value_sum], axis=0)
    both = jnp.broadcast_to(jnp.sum(both, axis=1, keepdims=True), (2 * dim, 2 * dim))
    sums[...] = both.T[:1]


def attend_back_call(lengths, qkv, bias, grad, heads, logs, after):
    ps, units, span = qkv.shape
    dim = units // 3
    shape = (ps, dim, span)
    rows = (ps * span, dim)
    vmem = pl.BlockSpec(memory_space=pltpu.VMEM)
    return pl.pallas_call(
        attend_back_body,
        in_specs=[SCALAR] + [vmem] * 5 + [ANY],
        out_specs=[vmem] * 2,
        out_shape=[
            jax.ShapeDtypeStruct((ps, units, span), BF16),
            jax.ShapeDtypeStruct((1, 2 * dim), F32),
        ],
        scratch_shapes=[
            pltpu.VMEM(shape, BF16),
            pltpu.VMEM(shape, BF16),
            pltpu.VMEM(rows, BF16),
            pltpu.VMEM(rows, BF16),
            pltpu.VMEM(rows, BF16),
            pltpu.VMEM(rows, BF16),
            pltpu.VMEM((ps, 1, span), F32),
            pltpu.VMEM(shape, F32),
        ],
        compiler_params=params(32),
        cost_estimate=cost(1),
        name="attend_back",
    )(lengths, qkv, bias, grad, heads, logs, after)


def out_body(place, heads, *refs):
    halves = refs[:HALVES]
    out, weight, blocks, sems = refs[HALVES:]
    dim, part = blocks.shape[1:]
    copies = load_halves(halves, blocks, sems, pl.ds(halves[0].shape[1] - dim, dim))
    for copy in copies:
        copy.start()
    flat = heads[...].reshape(heads.shape[0] * dim, heads.shape[2])
    for copy in copies:
        copy.wait()
    for j in range(8):
        for g in range(8):
            weight[j * dim : (j + 1) * dim, g * part : (g + 1) * part] = blocks[ring_slot(place, g, j)]
    out[...] = dot_tn(flat, weight[...]).astype(BF16)


def out_call(place, heads, halves):
    js, dim, rows = heads.shape
    part = halves[0].shape[2]
    width = 8 * part
    vmem = pl.BlockSpec(memory_space=pltpu.VMEM)
    return pl.pallas_call(
        out_body,
        in_specs=[SCALAR, vmem] + [ANY] * HALVES,
        out_specs=[vmem] * 2,
        out_shape=[
            jax.ShapeDtypeStruct((rows, width), BF16),
            jax.ShapeDtypeStruct((js * dim, width), BF16),
        ],
        scratch_shapes=[
            pltpu.VMEM((8 * js, dim, part), BF16),
            pltpu.SemaphoreType.DMA((HALVES,)),
        ],
        compiler_params=params(16),
        cost_estimate=cost(1),
        name="out",
    )(place, heads, *halves)


COLUMNS = 2


def feed_body(
    place, own, other, mine, theirs, out_shift, gain, shift, cot_own, cot_other, proj_shift, *refs
):
    halves = refs[:HALVES]
    base, share, grad_share, middle = refs[HALVES : HALVES + 4]
    grads = refs[HALVES + 4 : HALVES + 4 + NUM_SENT]
    normed, cot, acc, grad_acc, blocks, grad_blocks, sems = refs[HALVES + 4 + NUM_SENT :]
    step = pl.program_id(0)
    rows = own.shape[0]
    width = own.shape[1]
    part = blocks.shape[2]
    units = (blocks.shape[1] - EXTRA) // 2
    kept = 2 * units + EXTRA
    c = place[0]
    here = pl.ds(pl.multiple_of(c * rows, rows), rows)
    there = pl.ds(pl.multiple_of((1 - c) * rows, rows), rows)

    @pl.when(step == 0)
    def first():
        copies = load_halves(halves, blocks, sems, pl.ds(0, kept))
        for copy in copies:
            copy.start()
        middle[here, :] = own[...].astype(F32)
        middle[there, :] = other[...].astype(F32)
        cot[here, :] = cot_own[...]
        cot[there, :] = cot_other[...]
        values = middle[...] + (mine[...].astype(F32) + theirs[...].astype(F32)) + out_shift[...]
        middle[...] = values
        unit, unused = norm_parts(values)
        low = (unit * gain[...] + shift[...]).astype(BF16)
        normed[...] = low
        acc[...] = jnp.zeros_like(acc)
        grad_acc[...] = jnp.zeros_like(grad_acc)
        for copy in copies:
            copy.wait()

    pairs = [(step * COLUMNS + i, [ring_slot(place, g, step * COLUMNS + i) for g in range(8)]) for i in range(COLUMNS)]

    def rows_of(first):
        return jnp.concatenate(
            [
                jnp.concatenate([blocks[i, first : first + units, :] for i in spots], axis=1)
                for unused, spots in pairs
            ],
            axis=0,
        )

    fc, proj = rows_of(0), rows_of(units)
    lines = []
    for unused, spots in pairs:
        halves_of = blocks[spots[0], 2 * units : kept, :].astype(F32)
        for i in range(units // part):
            line = halves_of[3 * i : 3 * i + 1] + halves_of[3 * i + 1 : 3 * i + 2] + halves_of[3 * i + 2 : 3 * i + 3]
            lines.append(jnp.broadcast_to(line, (part, part)).T[:, :1])
    pre = dot_nt(fc, normed[...]) + jnp.concatenate(lines, axis=0)
    act_grad = dot_nt(proj, cot[...])
    root = 0.7978845608028654
    square = pre * pre
    bend = jnp.tanh(root * pre * (1.0 + 0.044715 * square))
    half = 0.5 * (1.0 + bend)
    activated = (pre * half).astype(BF16)
    slope = half + 0.5 * pre * (1.0 - bend * bend) * (root * (1.0 + 3 * 0.044715 * square))
    pre_grad = (act_grad * slope).astype(BF16)
    shift_grad = jnp.sum(pre_grad.astype(F32), axis=1, keepdims=True)
    acc[...] += dot_tn(activated, proj)
    grad_acc[...] += dot_tn(pre_grad, fc)
    fc_grad = dot(pre_grad, normed[...]).astype(BF16)
    proj_grad = dot(activated, cot[...]).astype(BF16)
    for n, (j, unused) in enumerate(pairs):
        mine_rows = slice(n * units, (n + 1) * units)
        extra = stack_halves(
            [
                jnp.broadcast_to(shift_grad[n * units + i * part : n * units + (i + 1) * part], (part, part)).T[:1]
                for i in range(units // part)
            ]
        )
        for g in range(8):
            i = slot(place, g, j, -1)
            lanes = slice(g * part, (g + 1) * part)
            grad_blocks[i, :units, :] = fc_grad[mine_rows, lanes]
            grad_blocks[i, units : 2 * units, :] = proj_grad[mine_rows, lanes]
            grad_blocks[i, 2 * units :, :] = extra

    @pl.when(step == pl.num_programs(0) - 1)
    def last():
        copies = store_blocks(grads, grad_blocks, sems)
        for copy in copies:
            copy.start()
        base[...] = middle[here, :] + acc[here, :] + proj_shift[...]
        share[...] = acc[there, :].astype(BF16)
        grad_share[...] = grad_acc[...].astype(BF16)
        for copy in copies:
            copy.wait()


def feed_call(place, own, other, mine, theirs, out_shift, gain, shift, cot_own, cot_other, proj_shift, halves):
    rows, width = own.shape
    unused, packed_rows, part = halves[0].shape
    kept = packed_rows - HEAD_DIM
    row = whole((1, width))
    some, all_rows = whole((rows, width)), whole((2 * rows, width))
    both = (2 * rows, width)
    return pl.pallas_call(
        feed_body,
        grid=(8 // COLUMNS,),
        in_specs=[SCALAR, some, some, all_rows, all_rows, row, row, row, some, some, row] + [ANY] * HALVES,
        out_specs=[some, some, all_rows, all_rows] + [ANY] * NUM_SENT,
        out_shape=[
            jax.ShapeDtypeStruct((rows, width), F32),
            jax.ShapeDtypeStruct((rows, width), BF16),
            jax.ShapeDtypeStruct(both, BF16),
            jax.ShapeDtypeStruct(both, F32),
        ]
        + sent_shapes(kept, part),
        scratch_shapes=[
            pltpu.VMEM(both, BF16),
            pltpu.VMEM(both, BF16),
            pltpu.VMEM(both, F32),
            pltpu.VMEM(both, F32),
            pltpu.VMEM((64, kept, part), BF16),
            pltpu.VMEM((64, kept, part), BF16),
            pltpu.SemaphoreType.DMA((HALVES,)),
        ],
        compiler_params=params(56),
        cost_estimate=cost(1),
        name="feed",
    )(place, own, other, mine, theirs, out_shift, gain, shift, cot_own, cot_other, proj_shift, *halves)


EXTRA = 16


def stack_halves(rows):
    place = lax.broadcasted_iota(jnp.int32, (EXTRA, rows[0].shape[1]), 0)
    block = jnp.zeros(place.shape, F32)
    for i, row in enumerate(rows):
        high = row.astype(BF16).astype(F32)
        block = jnp.where(place == 2 * i, high, block)
        block = jnp.where(place == 2 * i + 1, row - high, block)
    return block.astype(BF16)


def middle_body(
    place, middle, mine, theirs, gain, cot_own, cot_other, heads, weight,
    grad_own, out_grad, sums, weight_grad, cot, scaled,
):
    rows = cot_own.shape[0]
    c = place[0]
    here = pl.ds(pl.multiple_of(c * rows, rows), rows)
    there = pl.ds(pl.multiple_of((1 - c) * rows, rows), rows)
    cot[here, :] = cot_own[...].astype(F32)
    cot[there, :] = cot_other[...].astype(F32)
    unit, inverse = norm_parts(middle[...])
    grad = mine[...].astype(F32) + theirs[...].astype(F32)
    total = cot[...] + norm_back(grad, unit, inverse, gain[...])
    low = total.astype(BF16)
    cot[...] = total
    scaled[...] = grad * unit
    js, dim, span = heads.shape
    out_grad[...] = dot_nt(weight[...], low).astype(BF16).reshape(js, dim, span)
    weight_grad[...] = dot(heads[...].reshape(js * dim, span), low).astype(BF16).reshape(weight_grad.shape)
    kept = cot[here, :]
    grad_own[...] = kept
    sums[0:1, :] = jnp.sum(scaled[here, :], axis=0, keepdims=True)
    scaled[...] = grad
    sums[1:2, :] = jnp.sum(scaled[here, :], axis=0, keepdims=True)
    sums[2:3, :] = jnp.sum(kept, axis=0, keepdims=True)
    sums[3:4, :] = jnp.sum(cot_own[...].astype(F32), axis=0, keepdims=True)


def middle_call(place, middle, mine, theirs, gain, cot_own, cot_other, heads, weight):
    rows, width = cot_own.shape
    js, dim, span = heads.shape
    vmem = pl.BlockSpec(memory_space=pltpu.VMEM)
    return pl.pallas_call(
        middle_body,
        in_specs=[SCALAR] + [vmem] * 8,
        out_specs=[vmem] * 4,
        out_shape=[
            jax.ShapeDtypeStruct((rows, width), F32),
            jax.ShapeDtypeStruct(heads.shape, BF16),
            jax.ShapeDtypeStruct((4, width), F32),
            jax.ShapeDtypeStruct((js, dim, width), BF16),
        ],
        scratch_shapes=[pltpu.VMEM((2 * rows, width), F32)] * 2,
        compiler_params=params(56),
        cost_estimate=cost(1),
        name="middle",
    )(place, middle, mine, theirs, gain, cot_own, cot_other, heads, weight)


def qkv_back_body(place, grad, gain, shift, tokens_own, tokens_other, head_sums, early, out_grad, *refs):
    came = refs[:NUM_CAME]
    own, share, sums = refs[NUM_CAME + 1 : NUM_CAME + 4]
    grads = refs[NUM_CAME + 4 : NUM_CAME + 4 + NUM_SENT]
    acc, unit, normed, blocks, grad_blocks, load_sems, sems = refs[NUM_CAME + 4 + NUM_SENT :]
    step = pl.program_id(0)
    units, part = blocks.shape[1:]
    rows = own.shape[0]
    heads, unused, span = grad.shape
    dim = out_grad.shape[1]
    c = place[0]
    here = pl.ds(pl.multiple_of(c * rows, rows), rows)
    there = pl.ds(pl.multiple_of((1 - c) * rows, rows), rows)

    @pl.when(step == 0)
    def first():
        copies = load_blocks(came, blocks, load_sems)
        for copy in copies:
            copy.start()
        acc[...] = jnp.zeros_like(acc)
        unit[here, :], unused = norm_parts(tokens_own[...].astype(F32))
        unit[there, :], unused = norm_parts(tokens_other[...].astype(F32))
        normed[...] = (unit[...] * gain[...] + shift[...]).astype(BF16)
        for copy in copies:
            copy.wait()

    flat = grad[...].reshape(heads * units, span)
    product = dot(flat, normed[...]).astype(BF16)
    group = lax.rem(place[3], 2) * 4 + place[1]
    for n in range(heads):
        j = step * heads + n
        extra = stack_halves([jnp.where(group == j, head_sums[...], 0.0)])
        for g in range(8):
            i = slot(place, g, j, -1)
            lanes = slice(g * part, (g + 1) * part)
            grad_blocks[i, :units, :] = product[n * units : (n + 1) * units, lanes]
            grad_blocks[i, units : units + dim, :] = out_grad[n, :, lanes]
            grad_blocks[i, units + dim :, :] = extra

    @pl.when(step == pl.num_programs(0) - 1)
    def start_stores():
        for copy in store_blocks(grads, grad_blocks, sems):
            copy.start()

    acc[...] += dot_tn(flat, head_weights(place, blocks, step * heads, heads))

    @pl.when(step == pl.num_programs(0) - 1)
    def last():
        own[...] = acc[here, :]
        share[:rows, :] = acc[there, :].astype(BF16)
        sums[0:4, :] = early[...]
        sums[4:5, :] = jnp.sum(acc[...] * unit[...], axis=0, keepdims=True)
        sums[5:6, :] = jnp.sum(acc[...], axis=0, keepdims=True)
        sums[6:8, :] = jnp.zeros((2, sums.shape[1]), F32)
        share[rows:, :] = stack_halves([sums[i : i + 1, :] for i in range(6)])
        for copy in store_blocks(grads, grad_blocks, sems):
            copy.wait()


def qkv_back_call(place, grad, gain, shift, tokens_own, tokens_other, head_sums, early, out_grad, came, after):
    js, units, both = grad.shape
    part = came[0].shape[2]
    rows, width = tokens_own.shape
    heads = 4
    packed_rows = units + out_grad.shape[1] + EXTRA
    some = whole((rows, width))
    return pl.pallas_call(
        qkv_back_body,
        grid=(js // heads,),
        in_specs=[
            SCALAR,
            pl.BlockSpec((heads, units, both), lambda j: (j, 0, 0)),
            whole((1, width)),
            whole((1, width)),
            some,
            some,
            whole(head_sums.shape),
            whole(early.shape),
            pl.BlockSpec((heads,) + out_grad.shape[1:], lambda j: (j, 0, 0)),
        ]
        + [ANY] * (NUM_CAME + 1),
        out_specs=[some, whole((rows + EXTRA, width)), whole((8, width))] + [ANY] * NUM_SENT,
        out_shape=[
            jax.ShapeDtypeStruct((rows, width), F32),
            jax.ShapeDtypeStruct((rows + EXTRA, width), BF16),
            jax.ShapeDtypeStruct((8, width), F32),
        ]
        + sent_shapes(packed_rows, part),
        scratch_shapes=[
            pltpu.VMEM((both, width), F32),
            pltpu.VMEM((both, width), F32),
            pltpu.VMEM((both, width), BF16),
            pltpu.VMEM((64, units, part), BF16),
            pltpu.VMEM((64, packed_rows, part), BF16),
            pltpu.SemaphoreType.DMA((NUM_CAME,)),
            pltpu.SemaphoreType.DMA((NUM_SENT,)),
        ],
        compiler_params=params(56),
        cost_estimate=cost(1),
        name="qkv_back",
    )(place, grad, gain, shift, tokens_own, tokens_other, head_sums, early, out_grad, *came, after)


def input_body(own, share, sums, inputs, gain, middle_grad, out, total):
    rows = own.shape[0]
    unit, inverse = norm_parts(inputs[...].astype(F32))
    grad = own[...] + share[:rows, :].astype(F32)
    out[...] = middle_grad[...] + norm_back(grad, unit, inverse, gain[...])
    halves = share[rows:, :].astype(F32)
    for i in range(sums.shape[0]):
        total[i : i + 1, :] = sums[i : i + 1, :] + (halves[2 * i : 2 * i + 1] + halves[2 * i + 1 : 2 * i + 2])


def input_call(own, share, sums, inputs, gain, middle_grad):
    rows, width = own.shape
    vmem = pl.BlockSpec(memory_space=pltpu.VMEM)
    return pl.pallas_call(
        input_body,
        in_specs=[vmem] * 6,
        out_specs=[vmem] * 2,
        out_shape=[jax.ShapeDtypeStruct((rows, width), F32), jax.ShapeDtypeStruct(sums.shape, F32)],
        compiler_params=params(12),
        cost_estimate=cost(1),
        name="input",
    )(own, share, sums, inputs, gain, middle_grad)


def pack_body(w_qkv, w_fc, w_proj, w_out, shift, spread, feed):
    for i in range(spread.shape[0]):
        spread[i] = w_qkv[...]
    units, part = w_proj.shape
    feed[:units, :] = turn(w_fc[...])
    feed[units : 2 * units, :] = w_proj[...]
    place = lax.broadcasted_iota(jnp.int32, (EXTRA, part), 0)
    block = jnp.zeros(place.shape, F32)
    for n in range(units // part):
        rest = shift[:, n * part : (n + 1) * part]
        for i in range(3):
            high = rest.astype(BF16).astype(F32)
            block = jnp.where(place == 3 * n + i, high, block)
            rest = rest - high
    feed[2 * units : 2 * units + EXTRA, :] = block.astype(BF16)
    feed[2 * units + EXTRA :, :] = w_out[...]


def pack_call(w_qkv, w_fc, w_proj, w_out, shift):
    units, part = w_proj.shape
    vmem = pl.BlockSpec(memory_space=pltpu.VMEM)
    return pl.pallas_call(
        pack_body,
        in_specs=[vmem] * 5,
        out_specs=[vmem] * 2,
        out_shape=[
            jax.ShapeDtypeStruct((16,) + w_qkv.shape, BF16),
            jax.ShapeDtypeStruct((2 * units + EXTRA + w_out.shape[0], part), BF16),
        ],
        compiler_params=params(56),
        cost_estimate=cost(1),
        name="pack",
    )(w_qkv, w_fc, w_proj, w_out, shift)


def join_body(groups, *refs):
    ins, outs, sems = refs[: -len(groups) - 2], refs[-len(groups) - 1 : -1], refs[-1]
    copies = []
    for out, group in zip(outs, groups):
        at = 0
        for i, first, size in group:
            source = ins[i] if first is None else ins[i].at[pl.ds(first, size)]
            target = out.at[at] if first is None else out.at[pl.ds(at, size)]
            copies.append(pltpu.make_async_copy(source, target, sems.at[len(copies)]))
            at += size
    for copy in copies:
        copy.start()
    for copy in copies:
        copy.wait()


def join_call(arrays, groups, after):
    shape = arrays[0].shape if groups[0][0][1] is None else arrays[0].shape[1:]
    return pl.pallas_call(
        partial(join_body, groups),
        in_specs=[ANY] * (len(arrays) + 1),
        out_specs=[pl.BlockSpec(memory_space=pltpu.VMEM)] * len(groups),
        out_shape=[
            jax.ShapeDtypeStruct((sum(size for unused, unused_too, size in group),) + shape, BF16)
            for group in groups
        ],
        scratch_shapes=[pltpu.SemaphoreType.DMA((sum(len(group) for group in groups),))],
        compiler_params=params(6),
        cost_estimate=cost(1),
        name="join",
    )(*arrays, after)


def relay_body(left_low, right_high, from_left, from_right, after, sent_low, sent_high, token):
    token[...] = jnp.zeros_like(token)
    sent_low[...] = (left_low[...].astype(F32) + from_left[...].astype(F32)).astype(BF16)
    sent_high[...] = (right_high[...].astype(F32) + from_right[...].astype(F32)).astype(BF16)


def relay_call(left_low, right_high, from_left, from_right, after, mebibytes):
    vmem = pl.BlockSpec(memory_space=pltpu.VMEM)
    return pl.pallas_call(
        relay_body,
        in_specs=[vmem] * 4 + [ANY],
        out_specs=[vmem] * 3,
        out_shape=[jax.ShapeDtypeStruct(left_low.shape, BF16)] * 2 + [jax.ShapeDtypeStruct(TOKEN, F32)],
        compiler_params=params(mebibytes),
        cost_estimate=cost(1),
        name="relay",
    )(left_low, right_high, from_left, from_right, after)


def total_body(place, stays, got_low, got_high, more_low, more_high, after, *outs):
    at = jnp.where(place[0] == 0, place[2], place[3])
    for shift, out in enumerate(outs):
        w = lax.rem(at + shift, 4)
        for x in range(4):
            got, more = (got_low, more_low) if x < 2 else (got_high, more_high)
            i = x % 2 * 4 + w
            total = stays[x * 4 + w].astype(F32) + got[i].astype(F32) + more[i].astype(F32)
            out[x] = total.astype(BF16)


def total_call(place, stays, got_low, got_high, more_low, more_high, after):
    vmem = pl.BlockSpec(memory_space=pltpu.VMEM)
    return pl.pallas_call(
        total_body,
        in_specs=[SCALAR] + [vmem] * 5 + [ANY],
        out_specs=[vmem] * 4,
        out_shape=[jax.ShapeDtypeStruct((4,) + stays.shape[1:], BF16)] * 4,
        compiler_params=params(20),
        cost_estimate=cost(1),
        name="total",
    )(place, stays, got_low, got_high, more_low, more_high, after)


def next_body(place, one, two, three, four, after, *outs):
    for shift, out in enumerate(outs):
        x = lax.rem(place[1] + shift, 4)
        total = one[x].astype(F32) + two[x].astype(F32) + three[x].astype(F32) + four[x].astype(F32)
        out[...] = total.astype(BF16)


def next_call(place, arrays, after):
    vmem = pl.BlockSpec(memory_space=pltpu.VMEM)
    shape = arrays[0].shape[1:]
    return pl.pallas_call(
        next_body,
        in_specs=[SCALAR] + [vmem] * 4 + [ANY],
        out_specs=[vmem] * 4,
        out_shape=[jax.ShapeDtypeStruct(shape, BF16)] * 4,
        compiler_params=params(16),
        cost_estimate=cost(1),
        name="next",
    )(place, *arrays, after)


VECTORS = 6


def total_last_body(stays, got_low, got_high, more_low, more_high, one, two, three, four, after, out):
    size, rows, lanes = stays.shape
    vectors = (one[...] + two[...]) + (three[...] + four[...])
    wide = vectors.shape[1] // lanes
    count = VECTORS * wide
    place = lax.broadcasted_iota(jnp.int32, (2 * count, lanes), 0)
    block = jnp.zeros(place.shape, F32)
    for v in range(VECTORS):
        for k in range(wide):
            row = vectors[v : v + 1, k * lanes : (k + 1) * lanes]
            high = row.astype(BF16).astype(F32)
            block = jnp.where(place == v * wide + k, high, block)
            block = jnp.where(place == count + v * wide + k, row - high, block)
    block = block.astype(BF16)
    for i in range(size):
        got, more = (got_low, more_low) if i < size // 2 else (got_high, more_high)
        k = i % (size // 2)
        out[i, :rows, :] = (stays[i].astype(F32) + got[k].astype(F32) + more[k].astype(F32)).astype(BF16)
        out[i, rows:, :] = block


def total_last_call(stays, got_low, got_high, more_low, more_high, terms, after):
    size, rows, lanes = stays.shape
    more = 2 * VECTORS * terms[0].shape[1] // lanes
    vmem = pl.BlockSpec(memory_space=pltpu.VMEM)
    return pl.pallas_call(
        total_last_body,
        in_specs=[vmem] * 9 + [ANY],
        out_specs=vmem,
        out_shape=jax.ShapeDtypeStruct((size, rows + more, lanes), BF16),
        compiler_params=params(56),
        cost_estimate=cost(1),
        name="total_last",
    )(stays, got_low, got_high, more_low, more_high, *terms, after)


def gate_body(*refs):
    pass


def gate(arrays, after, mebibytes=1):
    return pl.pallas_call(
        gate_body,
        in_specs=[ANY] * (len(arrays) + 1),
        out_specs=[ANY] * len(arrays),
        out_shape=[jax.ShapeDtypeStruct(array.shape, array.dtype) for array in arrays],
        input_output_aliases={i: i for i in range(len(arrays))},
        compiler_params=params(mebibytes),
        cost_estimate=cost(1),
        name="gate",
    )(*arrays, after)


def sum_blocks(blocks):
    values = blocks[0].astype(F32)
    for i in range(1, blocks.shape[0]):
        values = values + blocks[i].astype(F32)
    return values


def feed_end_body(one, two, three, four, fc, proj, shift):
    total = one[...].astype(F32) + two[...].astype(F32) + three[...].astype(F32) + four[...].astype(F32)
    units, part = proj.shape
    fc[...] = total[:units].T
    proj[...] = total[units : 2 * units]
    for i in range(units // part):
        first = 2 * units + 2 * i
        shift[:, i * part : (i + 1) * part] = total[first : first + 1] + total[first + 1 : first + 2]


def feed_end_call(arrays, units):
    part = arrays[0].shape[1]
    vmem = pl.BlockSpec(memory_space=pltpu.VMEM)
    return pl.pallas_call(
        feed_end_body,
        in_specs=[vmem] * 4,
        out_specs=[vmem] * 3,
        out_shape=[
            jax.ShapeDtypeStruct((part, units), F32),
            jax.ShapeDtypeStruct((units, part), F32),
            jax.ShapeDtypeStruct((1, units), F32),
        ],
        compiler_params=params(12),
        cost_estimate=cost(1),
        name="feed_end",
    )(*arrays)


def qkv_end_body(blocks, weight, out, shift, *vectors):
    total = sum_blocks(blocks)
    units, part = weight.shape
    dim = out.shape[0]
    weight[...] = total[:units]
    out[...] = total[units : units + dim]
    kept = units + dim
    shift[...] = total[kept : kept + 1] + total[kept + 1 : kept + 2]
    wide = vectors[0].shape[1] // part
    count = VECTORS * wide
    first = kept + EXTRA
    for v in range(VECTORS):
        for k in range(wide):
            i = first + v * wide + k
            vectors[v][:, k * part : (k + 1) * part] = total[i : i + 1] + total[i + count : i + count + 1]


def qkv_end_call(blocks, dim, width):
    unused, rows, part = blocks.shape
    vmem = pl.BlockSpec(memory_space=pltpu.VMEM)
    return pl.pallas_call(
        qkv_end_body,
        in_specs=[vmem],
        out_specs=[vmem] * (3 + VECTORS),
        out_shape=[
            jax.ShapeDtypeStruct((rows - dim - EXTRA - 2 * VECTORS * width // part, part), F32),
            jax.ShapeDtypeStruct((dim, part), F32),
            jax.ShapeDtypeStruct((1, part), F32),
        ]
        + [jax.ShapeDtypeStruct((1, width), F32)] * VECTORS,
        compiler_params=params(12),
        cost_estimate=cost(1),
        name="qkv_end",
    )(blocks)


def swap(values):
    return lax.ppermute(values, "c", [(0, 1), (1, 0)])


def trade(values, names):
    return lax.all_to_all(values, names, 0, 0, tiled=True)


def device(x, y, z, c):
    return (((z // 2 * 4 + y) * 2 + z % 2) * 4 + x) * 2 + c


PLANES = [[device(x, y, z, 0) for x in range(4) for y in range(4)] for z in range(4)] + [
    [device(x, y, z, 1) for x in range(4) for z in range(4)] for y in range(4)
]


def trade_plane(values):
    return lax.all_to_all(values, EVERY, 0, 0, axis_index_groups=PLANES, tiled=True)


def move(values, shift, axes="zy"):
    pairs = []
    for x in range(4):
        for y in range(4):
            for z in range(4):
                for c in range(2):
                    to = {"x": x, "y": y, "z": z}
                    to[axes[c]] = (to[axes[c]] + shift) % 4
                    pairs.append((device(x, y, z, c), device(c=c, **to)))
    return lax.ppermute(values, EVERY, sorted(pairs))


def gather_ring(values, axes):
    return [values] + [move(values, shift, axes) for shift in (1, 2, 3)]


def on_device(
    tokens, ln1_gain, ln1_bias, w_qkv, b_qv, w_out, b_out, ln2_gain, ln2_bias,
    w_fc, b_fc, w_proj, b_proj, lengths, cotangent,
):
    place = jnp.stack(
        [
            lax.axis_index("c"),
            lax.axis_index("x"),
            lax.axis_index("y"),
            lax.axis_index("zh") * 2 + lax.axis_index("zl"),
        ]
    ).astype(jnp.int32)
    line = lambda vector: vector.reshape(1, -1)

    tokens_other = swap(tokens)
    cot_other = swap(cotangent)

    spread, feed_shard = pack_call(
        jnp.transpose(w_qkv, (1, 2, 0))[0], w_fc, w_proj, w_out[0], line(b_fc)
    )
    qkv_plane = trade_plane(spread)
    ones = gather_ring(feed_shard, "yz")
    one = join_call(ones, (tuple((i, None, 1) for i in range(4)),), feed_shard)[0]
    qkv_plane = gate([qkv_plane], one)[0]
    left, right, near, last, one_left = gate(
        [move(qkv_plane, 1), move(qkv_plane, 3), move(one, 1, "xx"), move(one, 3, "xx"), move(one, 1)], place
    )
    far_left, far, one_right, one_far = gate(
        [move(left, 1), move(near, 1, "xx"), move(one, 3), move(one_left, 1)], place
    )
    qkv_weight = [qkv_plane, left, far_left, right]

    qkv, token = qkv_call(
        place, tokens, tokens_other, line(ln1_gain), line(ln1_bias), qkv_weight, cot_other, far
    )
    low, high = join_call([near, far, last], (((0, 0, 4), (1, 0, 2)), ((1, 2, 2), (2, 0, 4))), token)
    qkv = trade(qkv, GROUP)
    low_left, high_right, high_left, low_right = move(low, 1), move(high, 3), move(high, 1), move(low, 3)
    heads, logs = attend_call(lengths, qkv, b_qv)
    head_out = heads
    low_left, high_right = gate([low_left, high_right], logs)
    feed_weight = [one, low, high, one_left, low_left, high_left]
    feed_weight += [one_far, move(low_left, 1), move(high_right, 3), one_right, low_right, high_right]
    heads = trade(heads, GROUP)
    mine, out_weight = out_call(place, heads, feed_weight)
    theirs = swap(mine)
    base, share, grad_mine, middle, *feed_grad = feed_call(
        place, tokens, tokens_other, mine, theirs, line(b_out), line(ln2_gain), line(ln2_bias),
        cotangent, cot_other, line(b_proj), feed_weight,
    )
    activations = (base + swap(share).astype(F32)).astype(BF16)
    grad_theirs = swap(grad_mine)
    far_low, far_high, left_low, left_high, right_low, right_high, stays = feed_grad
    from_left, from_right = move(far_low, 1), move(far_high, 3)
    middle_grad, out_grad, sums, out_weight_grad = middle_call(
        place, middle, grad_mine, grad_theirs, line(ln2_gain), cotangent, cot_other, heads, out_weight
    )
    sent_low, sent_high, token = relay_call(left_low, right_high, from_left, from_right, sums, 56)
    out_grad = trade(out_grad, GROUP)
    sent_low, sent_high = gate([sent_low, sent_high], out_grad)
    qkv_grad, head_sums = attend_back_call(lengths, qkv, b_qv, out_grad, head_out, logs, sent_low)
    got_high, got_low, more_low, more_high = gate(
        [move(left_high, 1), move(right_low, 3), move(sent_low, 1), move(sent_high, 3)], head_sums
    )
    qkv_grad = gate([qkv_grad], more_low)[0]
    steps = total_call(place, stays, got_low, got_high, more_low, more_high, head_sums)
    qkv_grad = trade(qkv_grad, GROUP)
    one, two, three = [move(steps[shift], shift, "yz") for shift in (1, 2, 3)]
    qkv_grad, one, three = gate([qkv_grad, one, three], head_sums)

    own, share_one, sums, far_low, far_high, left_low, left_high, right_low, right_high, stays = qkv_back_call(
        place, qkv_grad, line(ln1_gain), line(ln1_bias), tokens, tokens_other, head_sums, sums, out_weight_grad,
        qkv_weight, head_sums
    )
    steps = next_call(place, [steps[0], one, two, three], sums)
    feed_blocks = [steps[0]] + [move(steps[shift], shift, "xx") for shift in (1, 2, 3)]
    from_left, from_right = move(far_low, 1), move(far_high, 3)
    got_high, got_low = move(left_high, 1), move(right_low, 3)
    sent_low, sent_high, unused = relay_call(left_low, right_high, from_left, from_right, place, 56)
    more_low, more_high = move(sent_low, 1), move(sent_high, 3)
    input_grad, sums = input_call(own, swap(share_one), sums, tokens, line(ln1_gain), middle_grad)
    grad_w_fc, grad_w_proj, grad_b_fc = feed_end_call(feed_blocks, w_fc.shape[1])
    qkv_total = total_last_call(
        stays, got_low, got_high, more_low, more_high, gather_ring(sums, "zy"), grad_b_fc
    )
    qkv_blocks = trade_plane(qkv_total)
    grad_w_qkv, grad_w_out, grad_b_qv, *sums = qkv_end_call(qkv_blocks, w_out.shape[1], tokens.shape[1])
    return (
        activations,
        input_grad,
        sums[4].reshape(-1),
        sums[5].reshape(-1),
        jnp.transpose(grad_w_qkv[None], (2, 0, 1)),
        grad_b_qv,
        grad_w_out.reshape(w_out.shape),
        sums[2].reshape(-1),
        sums[0].reshape(-1),
        sums[1].reshape(-1),
        grad_w_fc,
        grad_b_fc.reshape(-1),
        grad_w_proj,
        sums[3].reshape(-1),
    )


def solution(mesh):
    chips = Mesh(mesh.devices.reshape(2, 4, 2, 4, 2), EVERY)
    gx, gy = ("zh", "y"), ("zl", "x", "c")
    in_specs = (
        P(EVERY, None),
        P(),
        P(),
        P(gx, gy, None),
        P(gy, None),
        P(gy, None, gx),
        P(),
        P(),
        P(),
        P(gx, gy),
        P(gy),
        P(gy, gx),
        P(),
        P(gx, None),
        P(EVERY, None),
    )
    out_specs = (
        P(EVERY, None),
        P(EVERY, None),
        P(),
        P(),
        P(gx, gy, None),
        P(gy, None),
        P(gy, None, gx),
        P(),
        P(),
        P(),
        P(gx, gy),
        P(gy),
        P(gy, gx),
        P(),
    )
    return jax.shard_map(
        on_device, mesh=chips, in_specs=in_specs, out_specs=out_specs, check_vma=False
    )
```
